1024 devices in a mesh: row: 16 (over z_hi, x, core), col: 64 (over y, z_lo).
Axes of the slice: x: 4, y: 8, z: 16 (z_hi: 2, z_lo: 8; z = z_hi * 8 + z_lo), core: 2. Of those that a mesh axis runs over, the one named last changes fastest.
Arguments:
- features: bfloat16 [131072, 256], P(('row', 'col')), may hold values from -6 to 6
- tile_values: int32 [16, 64, 10, 128, 128], P('row', 'col'), may hold values 0 or 1
- tile_block_row: int32 [16, 64, 10], P('row', 'col'), may hold values from 0 to 63
- tile_block_col: int32 [16, 64, 10], P('row', 'col'), may hold values from 0 to 15
- tile_count: int32 [16, 64], P('row', 'col'), may hold values from 8 to 10, as said below
- in_degree: int32 [131072], P(('row', 'col')), may hold values from 1 to 8
- w_self: bfloat16 [256, 256], replicated, may hold values from -0.375 to 0.375
- w_neigh: bfloat16 [256, 256], replicated, may hold values from -0.375 to 0.375
- bias: float32 [256], replicated, may hold values from -4 to 4
- grad_out: bfloat16 [131072, 256], P(('row', 'col')), may hold values from -6 to 6
Outputs:
- hidden: bfloat16 [131072, 256], P(('row', 'col'))
- grad_features: bfloat16 [131072, 256], P(('row', 'col'))
- grad_w_self: float32 [256, 256], replicated
- grad_w_neigh: float32 [256, 256], replicated
- grad_bias: float32 [256], replicated
The draws below stay inside these ranges and needn't reach their ends.
Inputs may be any that keep to these rules, and one draw needn't show every extreme that they name: `tile_count`: at least one grid block holds exactly 10 live slots.
All inputs are finite; a program needn't handle non-finite values. No bound on the sum of `tile_values` on one device may be relied on, other than what follows from the above.
Results may differ from the reference program's by a relative error of at most 0.007.
Values may be sent and summed in bfloat16 or wider, within the bound.
No kernel may reach another device: no remote copies, remote signals or barrier semaphores. Data moves between devices by JAX's collectives and lax.ppermute only.
A program may use at most 32 MiB of HBM per device.

```python
import jax
import jax.numpy as jnp
from jax import lax

HID = 256
TILE = 128
NODE_DEV = 128
TILE_SLOTS = 10
GRID_ROWS = 16
GRID_COLS = 64
NODES = 131072
DEST_TILES = 64
SRC_TILES = 16


def draw_tile_count(key, part):
    key = jax.random.fold_in(key, 7)
    first, second = jax.random.split(key)
    missing = jax.random.randint(first, (GRID_ROWS * GRID_COLS,), 0, TILE_SLOTS // 4 + 1)
    counts = (TILE_SLOTS - missing).astype(jnp.int32)
    chosen = jax.random.randint(second, (), 0, GRID_ROWS * GRID_COLS)
    counts = counts.at[chosen].set(TILE_SLOTS)
    return counts.reshape(GRID_ROWS, GRID_COLS).astype(jnp.int32)


def with_ends(entries, key, low, largest):
    extent = entries.shape
    place = [jax.random.randint(jax.random.fold_in(key, axis), (), 0, extent[axis]) for axis in range(len(extent))]
    entries = entries.at[tuple(place)].set(low)
    longest = extent.index(max(extent))
    place[longest] = (place[longest] + 1) % extent[longest]
    return entries.at[tuple(place)].set(largest)


def level_of(key, shape, cuts, low, high):
    loudness = 1.0
    for axis_at, parts in cuts:
        draws = jax.random.uniform(jax.random.fold_in(jax.random.fold_in(key, 6), axis_at), (parts,), jnp.float32, low / len(cuts), high / len(cuts))
        loudness = loudness * jnp.repeat(jnp.exp(draws), shape[axis_at] // parts).reshape((-1,) + (1,) * (len(shape) - 1 - axis_at))
    return loudness


def scatter_about(key, shape, deviation, limit, shards=(), kind=jnp.bfloat16):
    factor_of = level_of(key, shape, shards, -0.22, 0.18) if shards else 1.0
    values = jax.random.normal(key, shape, jnp.float32) * deviation * factor_of
    return jnp.minimum(jnp.maximum(values, -limit), limit).astype(kind)


def setup_inputs(seed: int = 0) -> dict:
    streams_of = jax.random.split(jax.random.key(seed), 11)
    return {
        "features": scatter_about(streams_of[0], (NODES, HID), 1.0, 6.0, ((0, 1024),)),
        "tile_values": with_ends((jax.random.randint(streams_of[1], (GRID_ROWS, GRID_COLS, TILE_SLOTS, TILE, TILE), 0, 160) < 1).astype(jnp.int32), jax.random.fold_in(streams_of[1], 1), 0, 1),
        "tile_block_row": with_ends(jax.random.randint(streams_of[2], (GRID_ROWS, GRID_COLS, TILE_SLOTS), 0, DEST_TILES), jax.random.fold_in(streams_of[2], 1), 0, DEST_TILES - 1).astype(jnp.int32),
        "tile_block_col": with_ends(jax.random.randint(streams_of[3], (GRID_ROWS, GRID_COLS, TILE_SLOTS), 0, SRC_TILES), jax.random.fold_in(streams_of[3], 1), 0, SRC_TILES - 1).astype(jnp.int32),
        "tile_count": draw_tile_count(jax.random.fold_in(streams_of[10], 71), 0),
        "in_degree": with_ends(jax.random.randint(streams_of[5], (NODES,), 1, 9), jax.random.fold_in(streams_of[5], 1), 1, 8).astype(jnp.int32),
        "w_self": scatter_about(streams_of[6], (HID, HID), HID ** -0.5, 0.375),
        "w_neigh": scatter_about(streams_of[7], (HID, HID), HID ** -0.5, 0.375),
        "bias": scatter_about(streams_of[8], (HID,), 1.0, 4.0, (), jnp.float32),
        "grad_out": scatter_about(streams_of[9], (NODES, HID), 1.0, 6.0, ((0, 1024),)),
    }


def activate(values):
    return jax.nn.gelu(values, approximate=True)

def reference(features, tile_values, tile_block_row, tile_block_col, tile_count, in_degree, w_self, w_neigh, bias, grad_out):
    block = NODE_DEV * GRID_COLS
    highest = lax.Precision.HIGHEST
    grid_feats = features.astype(jnp.float32).reshape(GRID_ROWS, GRID_COLS, NODE_DEV, HID)
    slots = jnp.arange(TILE_SLOTS, dtype=jnp.int32)

    def forward_step(carry, index):
        sums, counts = carry
        row_index = index // GRID_COLS
        col_index = index % GRID_COLS
        tiles = tile_values[row_index, col_index].astype(jnp.float32)
        panel = lax.dynamic_index_in_dim(grid_feats, col_index, 1, keepdims=False).reshape(SRC_TILES, TILE, HID)
        picked = panel[tile_block_col[row_index, col_index]]
        live = (slots < tile_count[row_index, col_index]).astype(jnp.float32)
        contrib = jnp.einsum('sij,sjf->sif', tiles, picked, precision=highest) * live[:, None, None]
        row_edges = lax.optimization_barrier(jnp.sum(tiles, axis=2)) * live[:, None]
        partial_value = jnp.zeros((DEST_TILES, TILE, HID), jnp.float32).at[tile_block_row[row_index, col_index]].add(contrib)
        edge_part = jnp.zeros((DEST_TILES, TILE), jnp.float32).at[tile_block_row[row_index, col_index]].add(row_edges)
        start = (row_index * block).astype(jnp.int32)
        current = lax.dynamic_slice_in_dim(sums, start, block, 0)
        sums = lax.dynamic_update_slice_in_dim(sums, current + partial_value.reshape(block, HID), start, 0)
        now_counts = lax.dynamic_slice_in_dim(counts, start, block, 0)
        counts = lax.dynamic_update_slice_in_dim(counts, now_counts + edge_part.reshape(block), start, 0)
        return ((sums, counts), None)
    indices = jnp.arange(GRID_ROWS * GRID_COLS, dtype=jnp.int32)
    init = (jnp.zeros((NODES, HID), jnp.float32), jnp.zeros((NODES,), jnp.float32))
    (neigh_sum, edge_counts), _ = lax.scan(forward_step, init, indices)
    degree = (edge_counts + in_degree.astype(jnp.float32))[:, None]
    aggregate = (neigh_sum / degree).astype(jnp.bfloat16)
    preact = jnp.dot(features, w_self, preferred_element_type=jnp.float32) + jnp.dot(aggregate, w_neigh, preferred_element_type=jnp.float32) + bias
    hidden, pullback = jax.vjp(activate, preact)
    grad_pre = pullback(grad_out.astype(jnp.float32))[0].astype(jnp.bfloat16)
    scaled_grad = (jnp.dot(grad_pre, w_neigh.T, preferred_element_type=jnp.float32) / degree).astype(jnp.bfloat16)
    scaled_wide = scaled_grad.astype(jnp.float32)

    def backward_step(carry, index):
        row_index = index // GRID_COLS
        col_index = index % GRID_COLS
        tiles = tile_values[row_index, col_index].astype(jnp.float32)
        start = (row_index * block).astype(jnp.int32)
        dest = lax.dynamic_slice_in_dim(scaled_wide, start, block, 0).reshape(DEST_TILES, TILE, HID)
        picked = dest[tile_block_row[row_index, col_index]]
        live = (slots < tile_count[row_index, col_index]).astype(jnp.float32)
        back = jnp.einsum('sij,sif->sjf', tiles, picked, precision=highest) * live[:, None, None]
        partial_value = jnp.zeros((SRC_TILES, TILE, HID), jnp.float32).at[tile_block_col[row_index, col_index]].add(back)
        partial_value = partial_value.reshape(GRID_ROWS, 1, NODE_DEV, HID)
        current = lax.dynamic_slice_in_dim(carry, col_index, 1, 1)
        return (lax.dynamic_update_slice_in_dim(carry, current + partial_value, col_index, 1), None)
    back_sum, _ = lax.scan(backward_step, jnp.zeros((GRID_ROWS, GRID_COLS, NODE_DEV, HID), jnp.float32), indices)
    grad_features = (jnp.dot(grad_pre, w_self.T, preferred_element_type=jnp.float32) + back_sum.reshape(NODES, HID)).astype(jnp.bfloat16)
    grad_w_self = jnp.dot(features.T, grad_pre, preferred_element_type=jnp.float32)
    grad_w_neigh = jnp.dot(aggregate.T, grad_pre, preferred_element_type=jnp.float32)
    grad_bias = lax.optimization_barrier(jnp.sum(grad_pre.astype(jnp.float32), axis=0))
    return (hidden.astype(jnp.bfloat16), grad_features, grad_w_self, grad_w_neigh, grad_bias)
```

```python
import functools

import jax
import jax.numpy as jnp
from jax import lax
from jax.experimental import pallas as pl
from jax.experimental.pallas import tpu as pltpu
from jax.sharding import Mesh, PartitionSpec as P

BF = jnp.bfloat16
F32 = jnp.float32
TILE = 128
HID = 256
QUAD = 4
CNT = 16
CHUNK = QUAD * TILE + CNT
VMEM = pl.BlockSpec(memory_space=pltpu.VMEM)
SMEM = pl.BlockSpec(memory_space=pltpu.SMEM)


def call(kernel, out, in_specs, *args, scratch=(), flops=0):
    shapes = [jax.ShapeDtypeStruct(s, t) for s, t in out]
    moved = sum(a.size * a.dtype.itemsize for a in args)
    moved += sum(s.size * s.dtype.itemsize for s in shapes)
    return pl.pallas_call(
        kernel,
        out_shape=shapes,
        in_specs=in_specs,
        out_specs=[VMEM] * len(shapes),
        scratch_shapes=list(scratch),
        compiler_params=pltpu.CompilerParams(vmem_limit_bytes=48 * 1024 * 1024),
        cost_estimate=pl.CostEstimate(flops=flops, bytes_accessed=moved, transcendentals=0),
    )(*args)


def split_counts(n):
    hi = n.astype(BF)
    lo = (n - hi.astype(F32)).astype(BF)
    return jnp.concatenate([hi, lo], axis=1)


def joined(block):
    return block[:, :TILE].astype(F32) + block[:, TILE:].astype(F32)


def row_counts(tile):
    ones = jnp.ones((8, TILE), BF)
    return lax.dot_general(ones, tile, (((1,), (1,)), ((), ())), preferred_element_type=F32)[0:1]


def add_counts(acc, chunk, lay, row):
    at = pl.multiple_of(chunk * CHUNK + QUAD * TILE, 16)
    mine = lax.broadcasted_iota(jnp.int32, (8, TILE), 0) == lay
    acc[pl.ds(at, 8), 0:TILE] += jnp.where(mine, jnp.broadcast_to(row, (8, TILE)), 0.0)


def contrib_kernel(slots, src, tiles, panel, msg, tiles_bf):
    msg[slots * TILE :, :] = jnp.zeros((CNT, HID), BF)
    rows = []
    for s in range(slots):
        tile = tiles[s].astype(F32).astype(BF)
        tiles_bf[s] = tile
        at = pl.multiple_of(src[s] * TILE, TILE)
        got = jnp.dot(tile, panel[pl.ds(at, TILE), :], preferred_element_type=F32)
        msg[s * TILE : (s + 1) * TILE, :] = got.astype(BF)
        rows.append(row_counts(tile))
    rows.append(jnp.zeros((CNT - slots, TILE), F32))
    counts = jnp.concatenate(rows, axis=0)
    msg[slots * TILE :, :] = jnp.concatenate([counts, jnp.zeros_like(counts)], axis=1).astype(BF)


def own_kernel(slots, src, idx, tiles, panel, acc):
    acc[...] = jnp.zeros_like(acc)
    for s in range(slots):

        @pl.when(idx[s] >= 0)
        def _():
            at = pl.multiple_of(src[s] * TILE, TILE)
            got = jnp.dot(tiles[s], panel[pl.ds(at, TILE), :], preferred_element_type=F32)
            chunk = idx[s] // QUAD
            lay = idx[s] % QUAD
            to = pl.multiple_of(chunk * CHUNK + lay * TILE, 16)
            acc[pl.ds(to, TILE), :] += got
            add_counts(acc, chunk, lay, row_counts(tiles[s]))


def merge_kernel(slots, chunks, idx, acc_in, recv, *refs):
    outs, acc = refs[:-1], refs[-1]
    acc[...] = acc_in[...]
    counts = recv[slots * TILE :, 0:TILE].astype(F32)
    for s in range(slots):

        @pl.when(idx[s] >= 0)
        def _():
            chunk = idx[s] // QUAD
            lay = idx[s] % QUAD
            to = pl.multiple_of(chunk * CHUNK + lay * TILE, 16)
            acc[pl.ds(to, TILE), :] += recv[s * TILE : (s + 1) * TILE, :].astype(F32)
            add_counts(acc, chunk, lay, counts[s : s + 1])

    for o in range(chunks):
        at = o * CHUNK
        outs[o][0 : QUAD * TILE, :] = acc[at : at + QUAD * TILE, :].astype(BF)
        outs[o][QUAD * TILE :, :] = split_counts(acc[at + QUAD * TILE : at + CHUNK, 0:TILE])


def add_kernel(recv, own, out):
    n = QUAD * TILE
    out[0:n, :] = (recv[0:n, :].astype(F32) + own[0:n, :].astype(F32)).astype(BF)
    out[n:, :] = split_counts(joined(recv[n:, :]) + joined(own[n:, :]))


def ring_end_kernel(*refs):
    parts, keep, send = refs[:-2], refs[-2], refs[-1]
    half, n = 2 * TILE, QUAD * TILE
    first = sum(p[0:half, :].astype(F32) for p in parts)
    second = sum(p[half:n, :].astype(F32) for p in parts)
    counts = sum(joined(p[n:, :]) for p in parts)
    keep[0:half, :] = first
    keep[half:, :] = jnp.concatenate([counts, counts], axis=1)
    send[0:half, :] = second.astype(BF)
    send[half:, :] = split_counts(counts)


def half_kernel(keep_in, recv, keep, send):
    half = 2 * TILE
    counts = keep_in[half : half + 8, 0:TILE] + joined(recv[half:, :])[2:10]
    counts = jnp.concatenate([counts, counts], axis=0)
    keep[0:TILE, :] = keep_in[0:TILE, :] + recv[0:TILE, :].astype(F32)
    keep[TILE:, :] = jnp.concatenate([counts, counts], axis=1)
    send[0:TILE, :] = (keep_in[TILE:half, :] + recv[TILE:half, :].astype(F32)).astype(BF)
    send[TILE:, :] = split_counts(counts)


def degree_column(row):
    eye = lax.broadcasted_iota(jnp.int32, (TILE, TILE), 0) == lax.broadcasted_iota(
        jnp.int32, (TILE, TILE), 1
    )
    wide = jnp.broadcast_to(row, (TILE, TILE))
    return jnp.sum(jnp.where(eye, wide, 0.0), axis=1, keepdims=True)


def node_kernel(
    keep, recv, in_degree, features, w_self, w_neigh, bias, grad_out, hidden, aggregate, grad_pre, scaled
):
    neigh = keep[0:TILE, :] + recv[0:TILE, :].astype(F32)
    edges = keep[TILE : TILE + 1, 0:TILE] + joined(recv[TILE:, :])[1:2]
    degree = degree_column(edges + in_degree[...].astype(F32))
    mean = (neigh / degree).astype(BF)
    aggregate[...] = mean
    v = (
        jnp.dot(features[...], w_self[...], preferred_element_type=F32)
        + jnp.dot(mean, w_neigh[...], preferred_element_type=F32)
        + bias[...]
    )
    c = 0.7978845608028654
    t = jnp.tanh(c * (v + 0.044715 * v * v * v))
    hidden[...] = (0.5 * v * (1.0 + t)).astype(BF)
    slope = 0.5 * (1.0 + t) + 0.5 * v * (1.0 - t * t) * (c * (1.0 + 3.0 * 0.044715 * v * v))
    g = (grad_out[...].astype(F32) * slope).astype(BF)
    grad_pre[...] = g
    back = lax.dot_general(g, w_neigh[...], (((1,), (1,)), ((), ())), preferred_element_type=F32)
    scaled[...] = (back / degree).astype(BF)


def weight_kernel(place, features, aggregate, grad_pre, w_self, keep, send, self_back):
    g = grad_pre[...]
    contract = (((0,), (0,)), ((), ()))
    first = lax.dot_general(features[...], g, contract, preferred_element_type=F32)
    second = lax.dot_general(aggregate[...], g, contract, preferred_element_type=F32)
    bias = jnp.broadcast_to(jnp.sum(g.astype(F32), axis=0, keepdims=True), (8, HID))
    mine = place[0] == 0
    keep[0:HID, :] = jnp.where(mine, first, second)
    send[0:HID, :] = jnp.where(mine, second, first)
    keep[HID:, :] = bias
    send[HID:, :] = bias
    self_back[...] = lax.dot_general(
        g, w_self[...], (((1,), (1,)), ((), ())), preferred_element_type=F32
    )


def weight_cut_kernel(size, place, keep_in, recv, *outs):
    rows = HID // size
    bias = keep_in[HID:, :] + recv[HID:, :]
    for d in range(size):
        at = pl.multiple_of(lax.rem(place[1] + d, size) * rows, 8)
        outs[d][0:rows, :] = keep_in[pl.ds(at, rows), :] + recv[pl.ds(at, rows), :]
        outs[d][rows:, :] = bias


def sum_kernel(*refs):
    refs[-1][...] = functools.reduce(lambda a, b: a + b, [r[...] for r in refs[:-1]])


def pick_kernel(slots, idx, local, msg):
    for s in range(slots):
        at = pl.multiple_of(jnp.maximum(idx[s], 0) * TILE, TILE)
        msg[s * TILE : (s + 1) * TILE, :] = local[pl.ds(at, TILE), :]


def back_kernel(slots, src, idx, live, tiles, local, recv, keep, send, acc, held):
    acc[...] = jnp.zeros_like(acc)
    for s in range(slots):

        @pl.when(live[s] > 0)
        def _():
            @pl.when(idx[s] >= 0)
            def _():
                at = pl.multiple_of(idx[s] * TILE, TILE)
                held[...] = local[pl.ds(at, TILE), :]

            @pl.when(idx[s] < 0)
            def _():
                held[...] = recv[s * TILE : (s + 1) * TILE, :]

            got = lax.dot_general(
                tiles[s], held[...], (((0,), (0,)), ((), ())), preferred_element_type=F32
            )
            to = pl.multiple_of(src[s] * TILE, TILE)
            acc[pl.ds(to, TILE), :] += got

    half = keep.shape[0]
    keep[...] = acc[0:half, :]
    send[...] = acc[half:, :].astype(BF)


def back_cut_kernel(keep_in, recv, keep, *sends):
    rows = keep.shape[0]
    for d, ref in enumerate((keep,) + sends):
        at = d * rows
        got = keep_in[at : at + rows, :] + recv[at : at + rows, :].astype(F32)
        ref[...] = got.astype(ref.dtype)


def back_gather_kernel(pieces, *refs):
    ins, outs = refs[: len(refs) - pieces], refs[len(refs) - pieces :]
    for d, ref in enumerate(outs):
        at = slice(d * TILE, (d + 1) * TILE)
        ref[...] = sum(r[at, :].astype(F32) for r in ins).astype(ref.dtype)


def body(
    features,
    tile_values,
    tile_block_row,
    tile_block_col,
    tile_count,
    in_degree,
    w_self,
    w_neigh,
    bias,
    grad_out,
):
    nh, nx, nk, ny, nl = (lax.axis_size(a) for a in ("h", "x", "k", "y", "l"))
    h, x, k, y, l = (lax.axis_index(a) for a in ("h", "x", "k", "y", "l"))
    slots = tile_values.shape[2]
    sources = nh * nx * nk

    def flip(value, axis, bit):
        n = lax.axis_size(axis)
        return lax.ppermute(value, axis, [(i, i ^ bit) for i in range(n)])

    def shift(value, axis, by):
        n = lax.axis_size(axis)
        return lax.ppermute(value, axis, [(i, (i + by) % n) for i in range(n)])

    slot = jnp.arange(slots, dtype=jnp.int32)
    live = (slot < tile_count[0, 0]).astype(jnp.int32)
    dest = jnp.where(live > 0, tile_block_row[0, 0], -1)
    source = tile_block_col[0, 0]
    sh, sx, sk = source // (nx * nk), (source // nk) % nx, source % nk
    src = (sk ^ k) * (nx * nh) + ((sx - x) % nx) * nh + (sh ^ h)

    def place(d):
        dl = d % nl
        far = (dl >> 1) ^ (l >> 1)
        lay = ((far & 1) << 1) | (far >> 1)
        at = ((d // nl - y) % ny) * QUAD + lay
        return jnp.where((d >= 0) & ((dl & 1) == (l & 1)), at, -1)

    meta = jnp.zeros((8, TILE), jnp.int32).at[0, :slots].set(dest)
    other = flip(meta, "l", 1)[0, :slots]
    own_idx, other_idx = place(dest), place(other)

    panel = features
    if nh > 1:
        panel = jnp.concatenate([panel, flip(panel, "h", 1)], axis=0)
    panel = jnp.concatenate([panel] + [shift(panel, "x", -d) for d in range(1, nx)], axis=0)
    panel = jnp.concatenate([panel, flip(panel, "k", 1)], axis=0)

    tile_flops = 2 * slots * TILE * TILE * HID
    msg, tiles = call(
        functools.partial(contrib_kernel, slots),
        [((slots * TILE + CNT, HID), BF), ((slots, TILE, TILE), BF)],
        [SMEM, VMEM, VMEM],
        src,
        tile_values[0, 0],
        panel,
        flops=tile_flops,
    )
    got = flip(msg, "l", 1)
    (acc,) = call(
        functools.partial(own_kernel, slots),
        [((ny * CHUNK, HID), F32)],
        [SMEM, SMEM, VMEM, VMEM],
        src,
        own_idx,
        tiles,
        panel,
        flops=tile_flops,
    )
    chunks = call(
        functools.partial(merge_kernel, slots, ny),
        [((CHUNK, HID), BF)] * ny,
        [SMEM, VMEM, VMEM],
        other_idx,
        acc,
        got,
        scratch=[pltpu.VMEM((ny * CHUNK, HID), F32)],
    )

    ups, downs = ny // 2, ny - 1 - ny // 2
    up, down = chunks[ups], chunks[(-downs) % ny]
    parts = [chunks[0]]
    for step in range(1, ups + 1):
        up = shift(up, "y", 1)
        if step <= downs:
            down = shift(down, "y", -1)
        if step < ups:
            (up,) = call(add_kernel, [((CHUNK, HID), BF)], [VMEM] * 2, up, chunks[ups - step])
        if step < downs:
            (down,) = call(
                add_kernel, [((CHUNK, HID), BF)], [VMEM] * 2, down, chunks[ny - downs + step]
            )
    parts.append(up)
    if downs:
        parts.append(down)
    half_rows, last_rows = 2 * TILE + CNT, TILE + CNT
    keep, send = call(
        ring_end_kernel,
        [((half_rows, HID), F32), ((half_rows, HID), BF)],
        [VMEM] * len(parts),
        *parts,
    )
    keep, send = call(
        half_kernel,
        [((last_rows, HID), F32), ((last_rows, HID), BF)],
        [VMEM] * 2,
        keep,
        flip(send, "l", 2),
    )
    node = ((TILE, HID), BF)
    hidden, aggregate, grad_pre, scaled = call(
        node_kernel,
        [node] * 4,
        [VMEM] * 8,
        keep,
        flip(send, "l", 4),
        in_degree.reshape(1, TILE),
        features,
        w_self,
        w_neigh,
        bias.reshape(1, HID),
        grad_out,
        flops=6 * TILE * HID * HID,
    )

    local = jnp.concatenate([scaled, flip(scaled, "l", 4)], axis=0)
    local = jnp.concatenate([local, flip(local, "l", 2)], axis=0)
    blocks = {0: local}
    up = down = local
    for step in range(1, ups + 1):
        up = shift(up, "y", 1)
        blocks[(-step) % ny] = up
        if step <= downs:
            down = shift(down, "y", -1)
            blocks[step] = down

    where = jnp.stack([k, x]).astype(jnp.int32)
    wide = ((HID + 8, HID), F32)
    w_keep, w_send, self_back = call(
        weight_kernel,
        [wide, wide, ((TILE, HID), F32)],
        [SMEM] + [VMEM] * 4,
        where,
        features,
        aggregate,
        grad_pre,
        w_self,
        flops=6 * TILE * HID * HID,
    )
    w_rows = HID // nx
    cut = ((w_rows + 8, HID), F32)
    cuts = call(
        functools.partial(weight_cut_kernel, nx),
        [cut] * nx,
        [SMEM, VMEM, VMEM],
        where,
        w_keep,
        flip(w_send, "k", 1),
    )
    got = [cuts[0]] + [shift(cuts[d], "x", d) for d in range(1, nx)]
    (total,) = call(sum_kernel, [cut], [VMEM] * nx, *got)
    for axis in ("y", "l", "h"):
        bit = 1
        while bit < lax.axis_size(axis):
            total = total + flip(total, axis, bit)
            bit *= 2
    grad_bias = total[w_rows]
    piece = total[:w_rows]
    whole = jnp.zeros((HID, HID), F32)
    for d in range(nx):
        part = piece if d == 0 else shift(piece, "x", -d)
        whole = lax.dynamic_update_slice(whole, part, (((x + d) % nx) * w_rows, 0))
    across = flip(whole, "k", 1)
    grad_w_self = jnp.where(k == 0, whole, across)
    grad_w_neigh = jnp.where(k == 0, across, whole)

    local = jnp.concatenate([blocks[o] for o in range(ny)], axis=0)
    (msg,) = call(
        functools.partial(pick_kernel, slots),
        [((slots * TILE, HID), BF)],
        [SMEM, VMEM],
        other_idx,
        local,
    )
    half = sources // 2 * TILE
    keep, send = call(
        functools.partial(back_kernel, slots),
        [((half, HID), F32), ((half, HID), BF)],
        [SMEM, SMEM, SMEM, VMEM, VMEM, VMEM],
        src,
        own_idx,
        live,
        tiles,
        local,
        flip(msg, "l", 1),
        scratch=[pltpu.VMEM((sources * TILE, HID), F32), pltpu.VMEM((TILE, HID), BF)],
        flops=tile_flops,
    )
    group = nh * TILE
    pieces = call(
        back_cut_kernel,
        [((group, HID), F32)] + [((group, HID), BF)] * (nx - 1),
        [VMEM] * 2,
        keep,
        flip(send, "k", 1),
    )
    got = [pieces[0]] + [shift(pieces[d], "x", d) for d in range(1, nx)]
    last = call(
        functools.partial(back_gather_kernel, nh),
        [((TILE, HID), F32)] + [((TILE, HID), BF)] * (nh - 1),
        [VMEM] * nx,
        *got,
    )
    back_sum = last[0]
    if nh > 1:
        back_sum = back_sum + flip(last[1], "h", 1).astype(F32)
    grad_features = (self_back + back_sum).astype(BF)
    return hidden, grad_features, grad_w_self, grad_w_neigh, grad_bias


def on_mesh(mesh):
    row, col = ("h", "x", "k"), ("y", "l")
    nodes = P(row + col, None)
    in_specs = (
        nodes,
        P(row, col, None, None, None),
        P(row, col, None),
        P(row, col, None),
        P(row, col),
        P(row + col),
        P(),
        P(),
        P(),
        nodes,
    )
    out_specs = (nodes, nodes, P(), P(), P())
    return jax.shard_map(body, mesh=mesh, in_specs=in_specs, out_specs=out_specs, check_vma=False)


def solution(mesh):
    devices = mesh.devices.reshape(2, 4, 2, 8, 8)
    return on_mesh(Mesh(devices, ("h", "x", "k", "y", "l")))
```

```python
import functools

import jax
import jax.numpy as jnp
from jax import lax
from jax.experimental import pallas as pl
from jax.experimental.pallas import tpu as pltpu
from jax.sharding import Mesh, PartitionSpec as P

BF = jnp.bfloat16
F32 = jnp.float32
TILE = 128
HID = 256
QUAD = 4
CNT = 16
CHUNK = QUAD * TILE + CNT
VMEM = pl.BlockSpec(memory_space=pltpu.VMEM)
SMEM = pl.BlockSpec(memory_space=pltpu.SMEM)
AFTER = pl.BlockSpec(memory_space=pl.ANY)


def call(kernel, out, in_specs, *args, scratch=(), flops=0):
    shapes = [jax.ShapeDtypeStruct(s, t) for s, t in out]
    moved = sum(a.size * a.dtype.itemsize for a in args)
    moved += sum(s.size * s.dtype.itemsize for s in shapes)
    return pl.pallas_call(
        kernel,
        out_shape=shapes,
        in_specs=in_specs,
        out_specs=[VMEM] * len(shapes),
        scratch_shapes=list(scratch),
        compiler_params=pltpu.CompilerParams(vmem_limit_bytes=48 * 1024 * 1024),
        cost_estimate=pl.CostEstimate(flops=flops, bytes_accessed=moved, transcendentals=0),
    )(*args)


def split_counts(n):
    hi = n.astype(BF)
    lo = (n - hi.astype(F32)).astype(BF)
    return jnp.concatenate([hi, lo], axis=1)


def joined(block):
    return block[:, :TILE].astype(F32) + block[:, TILE:].astype(F32)


def row_counts(tile):
    ones = jnp.ones((8, TILE), BF)
    return lax.dot_general(ones, tile, (((1,), (1,)), ((), ())), preferred_element_type=F32)[0:1]


def add_counts(acc, chunk, lay, row):
    at = pl.multiple_of(chunk * CHUNK + QUAD * TILE, 16)
    mine = lax.broadcasted_iota(jnp.int32, (8, TILE), 0) == lay
    acc[pl.ds(at, 8), 0:TILE] += jnp.where(mine, jnp.broadcast_to(row, (8, TILE)), 0.0)


def contrib_kernel(slots, src, tiles, panel, msg, tiles_bf):
    rows = []
    for s in range(slots):
        tile = tiles[s].astype(F32).astype(BF)
        tiles_bf[s] = tile
        at = pl.multiple_of(src[s] * TILE, TILE)
        got = jnp.dot(tile, panel[pl.ds(at, TILE), :], preferred_element_type=F32)
        msg[s * TILE : (s + 1) * TILE, :] = got.astype(BF)
        rows.append(row_counts(tile))
    rows.append(jnp.zeros((CNT - slots, TILE), F32))
    counts = jnp.concatenate(rows, axis=0)
    msg[slots * TILE :, :] = jnp.concatenate([counts, jnp.zeros_like(counts)], axis=1).astype(BF)


def merge_kernel(slots, chunks, src, idx, other_idx, tiles, panel, recv, *refs):
    outs, acc = refs[:-1], refs[-1]
    acc[...] = jnp.zeros_like(acc)
    counts = recv[slots * TILE :, 0:TILE].astype(F32)

    def put(at, tile, row):
        chunk = at // QUAD
        lay = at % QUAD
        to = pl.multiple_of(chunk * CHUNK + lay * TILE, 16)
        acc[pl.ds(to, TILE), :] += tile
        add_counts(acc, chunk, lay, row)

    for s in range(slots):

        @pl.when(idx[s] >= 0)
        def _():
            at = pl.multiple_of(src[s] * TILE, TILE)
            got = jnp.dot(tiles[s], panel[pl.ds(at, TILE), :], preferred_element_type=F32)
            put(idx[s], got, row_counts(tiles[s]))

        @pl.when(other_idx[s] >= 0)
        def _():
            put(
                other_idx[s], recv[s * TILE : (s + 1) * TILE, :].astype(F32), counts[s : s + 1]
            )

    for o in range(chunks):
        at = o * CHUNK
        outs[o][0 : QUAD * TILE, :] = acc[at : at + QUAD * TILE, :].astype(BF)
        outs[o][QUAD * TILE :, :] = split_counts(acc[at + QUAD * TILE : at + CHUNK, 0:TILE])


def add_kernel(recv, own, out):
    n = QUAD * TILE
    out[0:n, :] = (recv[0:n, :].astype(F32) + own[0:n, :].astype(F32)).astype(BF)
    out[n:, :] = split_counts(joined(recv[n:, :]) + joined(own[n:, :]))


def ring_end_kernel(*refs):
    parts, keep, send = refs[:-2], refs[-2], refs[-1]
    half, n = 2 * TILE, QUAD * TILE
    first = sum(p[0:half, :].astype(F32) for p in parts)
    second = sum(p[half:n, :].astype(F32) for p in parts)
    counts = sum(joined(p[n:, :]) for p in parts)
    keep[0:half, :] = first
    keep[half:, :] = jnp.concatenate([counts, counts], axis=1)
    send[0:half, :] = second.astype(BF)
    send[half:, :] = split_counts(counts)


def half_kernel(keep_in, recv, keep, send):
    half = 2 * TILE
    counts = keep_in[half : half + 8, 0:TILE] + joined(recv[half:, :])[2:10]
    counts = jnp.concatenate([counts, counts], axis=0)
    keep[0:TILE, :] = keep_in[0:TILE, :] + recv[0:TILE, :].astype(F32)
    keep[TILE:, :] = jnp.concatenate([counts, counts], axis=1)
    send[0:TILE, :] = (keep_in[TILE:half, :] + recv[TILE:half, :].astype(F32)).astype(BF)
    send[TILE:, :] = split_counts(counts)


def degree_column(row):
    eye = lax.broadcasted_iota(jnp.int32, (TILE, TILE), 0) == lax.broadcasted_iota(
        jnp.int32, (TILE, TILE), 1
    )
    wide = jnp.broadcast_to(row, (TILE, TILE))
    return jnp.sum(jnp.where(eye, wide, 0.0), axis=1, keepdims=True)


def node_kernel(
    keep, recv, in_degree, features, w_self, w_neigh, bias, grad_out,
    hidden, aggregate, grad_pre, scaled,
):
    neigh = keep[0:TILE, :] + recv[0:TILE, :].astype(F32)
    edges = keep[TILE : TILE + 1, 0:TILE] + joined(recv[TILE:, :])[1:2]
    degree = degree_column(edges + in_degree[...].astype(F32))
    mean = (neigh / degree).astype(BF)
    aggregate[...] = mean
    v = (
        jnp.dot(features[...], w_self[...], preferred_element_type=F32)
        + jnp.dot(mean, w_neigh[...], preferred_element_type=F32)
        + bias[...]
    )
    c = 0.7978845608028654
    t = jnp.tanh(c * (v + 0.044715 * v * v * v))
    hidden[...] = (0.5 * v * (1.0 + t)).astype(BF)
    slope = 0.5 * (1.0 + t) + 0.5 * v * (1.0 - t * t) * (c * (1.0 + 3.0 * 0.044715 * v * v))
    g = (grad_out[...].astype(F32) * slope).astype(BF)
    grad_pre[...] = g
    back = lax.dot_general(g, w_neigh[...], (((1,), (1,)), ((), ())), preferred_element_type=F32)
    scaled[...] = (back / degree).astype(BF)


def weight_kernel(place, features, aggregate, grad_pre, w_self, keep, send, self_back):
    g = grad_pre[...]
    contract = (((0,), (0,)), ((), ()))
    first = lax.dot_general(features[...], g, contract, preferred_element_type=F32)
    second = lax.dot_general(aggregate[...], g, contract, preferred_element_type=F32)
    bias = jnp.broadcast_to(jnp.sum(g.astype(F32), axis=0, keepdims=True), (8, HID))
    mine = place[0] == 0
    keep[0:HID, :] = jnp.where(mine, first, second)
    send[0:HID, :] = jnp.where(mine, second, first)
    keep[HID:, :] = bias
    send[HID:, :] = bias
    self_back[...] = lax.dot_general(
        g, w_self[...], (((1,), (1,)), ((), ())), preferred_element_type=F32
    )


def weight_cut_kernel(size, place, keep_in, recv, *outs):
    rows = HID // size
    bias = keep_in[HID:, :] + recv[HID:, :]
    for d in range(size):
        at = pl.multiple_of(lax.rem(place[1] + d, size) * rows, 8)
        outs[d][0:rows, :] = keep_in[pl.ds(at, rows), :] + recv[pl.ds(at, rows), :]
        outs[d][rows:, :] = bias


def sum_kernel(*refs):
    refs[-1][...] = functools.reduce(lambda a, b: a + b, [r[...] for r in refs[:-1]])


def whole_kernel(rows, place, own, *refs):
    recvs, whole = refs[:-1], refs[-1]
    size = len(recvs) + 1
    for d in range(size):
        at = lax.rem(place[1] + size - d, size)
        block = own if d == 0 else recvs[d - 1]
        whole[pl.ds(pl.multiple_of(at * rows, 8), rows), :] = block[0:rows, :]

        @pl.when(at == 0)
        def _():
            whole[HID:, :] = block[rows:, :]


def pick_kernel(slots, idx, local, after, msg):
    for s in range(slots):
        at = pl.multiple_of(jnp.maximum(idx[s], 0) * TILE, TILE)
        msg[s * TILE : (s + 1) * TILE, :] = local[pl.ds(at, TILE), :]


def back_kernel(slots, src, idx, live, tiles, recv, local, after, keep, send, acc, got):
    acc[...] = jnp.zeros_like(acc)
    for s in range(slots):

        @pl.when(live[s] > 0)
        def _():
            @pl.when(idx[s] >= 0)
            def _():
                at = pl.multiple_of(idx[s] * TILE, TILE)
                got[...] = local[pl.ds(at, TILE), :]

            @pl.when(idx[s] < 0)
            def _():
                got[...] = recv[s * TILE : (s + 1) * TILE, :]

            term = lax.dot_general(
                tiles[s], got[...], (((0,), (0,)), ((), ())), preferred_element_type=F32
            )
            to = pl.multiple_of(src[s] * TILE, TILE)
            acc[pl.ds(to, TILE), :] += term

    half = keep.shape[0]
    keep[...] = acc[0:half, :]
    send[...] = acc[half:, :].astype(BF)


def back_cut_kernel(keep_in, recv, total, passed, keep, *sends):
    passed[...] = total[...]
    rows = keep.shape[0]
    for d, ref in enumerate((keep,) + sends):
        at = d * rows
        got = keep_in[at : at + rows, :] + recv[at : at + rows, :].astype(F32)
        ref[...] = got.astype(ref.dtype)


def back_gather_kernel(count, total, *refs):
    ins, passed, outs = refs[:count], refs[count], refs[count + 1 :]
    passed[...] = total[...]
    for d, ref in enumerate(outs):
        at = slice(d * TILE, (d + 1) * TILE)
        ref[...] = sum(r[at, :].astype(F32) for r in ins).astype(ref.dtype)


def body(
    features,
    tile_values,
    tile_block_row,
    tile_block_col,
    tile_count,
    in_degree,
    w_self,
    w_neigh,
    bias,
    grad_out,
):
    nh, nx, nk, ny, nl = (lax.axis_size(a) for a in ("h", "x", "k", "y", "l"))
    h, x, k, y, l = (lax.axis_index(a) for a in ("h", "x", "k", "y", "l"))
    slots = tile_values.shape[2]
    sources = nh * nx * nk

    def flip(value, axis, bit):
        n = lax.axis_size(axis)
        return lax.ppermute(value, axis, [(i, i ^ bit) for i in range(n)])

    def shift(value, axis, by):
        n = lax.axis_size(axis)
        return lax.ppermute(value, axis, [(i, (i + by) % n) for i in range(n)])

    slot = jnp.arange(slots, dtype=jnp.int32)
    live = (slot < tile_count[0, 0]).astype(jnp.int32)
    dest = jnp.where(live > 0, tile_block_row[0, 0], -1)
    source = tile_block_col[0, 0]
    sh, sx, sk = source // (nx * nk), (source // nk) % nx, source % nk
    src = ((sk ^ k) * nx + (sx - x) % nx) * nh + (sh ^ h)

    def place(d):
        dl = d % nl
        far = (dl >> 1) ^ (l >> 1)
        lay = ((far & 1) << 1) | (far >> 1)
        mine = (d >= 0) & ((dl & 1) == (l & 1))
        ring = jnp.where(mine, ((d // nl - y) % ny) * QUAD + lay, -1)
        return ring, jnp.where(mine, (d // nl) * QUAD + lay, -1)

    meta = jnp.zeros((8, TILE), jnp.int32).at[0, :slots].set(dest)
    other = flip(meta, "l", 1)[0, :slots]
    own_ring, own_idx = place(dest)
    other_ring, other_idx = place(other)
    where = jnp.stack([k, x, y]).astype(jnp.int32)

    panel = features
    if nh > 1:
        panel = jnp.concatenate([panel, flip(panel, "h", 1)], axis=0)
    panel = jnp.concatenate([panel] + [shift(panel, "x", -d) for d in range(1, nx)], axis=0)
    panel = jnp.concatenate([panel, flip(panel, "k", 1)], axis=0)

    tile_flops = 2 * slots * TILE * TILE * HID
    msg, tiles = call(
        functools.partial(contrib_kernel, slots),
        [((slots * TILE + CNT, HID), BF), ((slots, TILE, TILE), BF)],
        [SMEM, VMEM, VMEM],
        src,
        tile_values[0, 0],
        panel,
        flops=tile_flops,
    )
    chunks = call(
        functools.partial(merge_kernel, slots, ny),
        [((CHUNK, HID), BF)] * ny,
        [SMEM, SMEM, SMEM, VMEM, VMEM, VMEM],
        src,
        own_ring,
        other_ring,
        tiles,
        panel,
        flip(msg, "l", 1),
        scratch=[pltpu.VMEM((ny * CHUNK, HID), F32)],
        flops=tile_flops,
    )

    ups, downs = ny // 2, ny - 1 - ny // 2
    up, down = chunks[ups], chunks[(-downs) % ny]
    parts = [chunks[0]]
    for step in range(1, ups + 1):
        up = shift(up, "y", 1)
        if step <= downs:
            down = shift(down, "y", -1)
        if step < ups:
            (up,) = call(add_kernel, [((CHUNK, HID), BF)], [VMEM] * 2, up, chunks[ups - step])
        if step < downs:
            (down,) = call(
                add_kernel, [((CHUNK, HID), BF)], [VMEM] * 2, down, chunks[ny - downs + step]
            )
    parts.append(up)
    if downs:
        parts.append(down)
    half_rows, last_rows = 2 * TILE + CNT, TILE + CNT
    keep, send = call(
        ring_end_kernel,
        [((half_rows, HID), F32), ((half_rows, HID), BF)],
        [VMEM] * len(parts),
        *parts,
    )
    keep, send = call(
        half_kernel,
        [((last_rows, HID), F32), ((last_rows, HID), BF)],
        [VMEM] * 2,
        keep,
        flip(send, "l", 2),
    )
    node = ((TILE, HID), BF)
    hidden, aggregate, grad_pre, scaled = call(
        node_kernel,
        [node] * 4,
        [VMEM] * 8,
        keep,
        flip(send, "l", 4),
        in_degree.reshape(1, TILE),
        features,
        w_self,
        w_neigh,
        bias.reshape(1, HID),
        grad_out,
        flops=6 * TILE * HID * HID,
    )

    local = jnp.concatenate([scaled, flip(scaled, "l", 4)], axis=0)
    local = jnp.concatenate([local, flip(local, "l", 2)], axis=0)
    local = lax.all_gather(local, "y", axis=0, tiled=True)

    wide = ((HID + 8, HID), F32)
    w_keep, w_send, self_back = call(
        weight_kernel,
        [wide, wide, ((TILE, HID), F32)],
        [SMEM] + [VMEM] * 4,
        where,
        features,
        aggregate,
        grad_pre,
        w_self,
        flops=6 * TILE * HID * HID,
    )
    w_rows = HID // nx
    cut = ((w_rows + 8, HID), F32)
    cuts = call(
        functools.partial(weight_cut_kernel, nx),
        [cut] * nx,
        [SMEM, VMEM, VMEM],
        where,
        w_keep,
        flip(w_send, "k", 1),
    )
    cuts = [cuts[0]] + [shift(cuts[d], "x", d) for d in range(1, nx)]
    (total,) = call(sum_kernel, [cut], [VMEM] * nx, *cuts)

    def add_over(value, axis, bit):
        return value + flip(value, axis, bit) if bit < lax.axis_size(axis) else value

    for bit in (1, 2, 4):
        total = add_over(total, "l", bit)

    (msg,) = call(
        functools.partial(pick_kernel, slots),
        [((slots * TILE, HID), BF)],
        [SMEM, VMEM, AFTER],
        other_idx,
        local,
        total,
    )
    total = add_over(add_over(total, "y", 1), "y", 2)
    half = sources // 2 * TILE
    keep, send = call(
        functools.partial(back_kernel, slots),
        [((half, HID), F32), ((half, HID), BF)],
        [SMEM, SMEM, SMEM, VMEM, VMEM, VMEM, AFTER],
        src,
        own_idx,
        live,
        tiles,
        flip(msg, "l", 1),
        local,
        total,
        scratch=[pltpu.VMEM((sources * TILE, HID), F32), pltpu.VMEM((TILE, HID), BF)],
        flops=tile_flops,
    )
    group = nh * TILE
    total, *pieces = call(
        back_cut_kernel,
        [cut, ((group, HID), F32)] + [((group, HID), BF)] * (nx - 1),
        [VMEM] * 3,
        keep,
        flip(send, "k", 1),
        add_over(total, "y", 4),
    )
    got = [pieces[0]] + [shift(pieces[d], "x", d) for d in range(1, nx)]
    total, *last = call(
        functools.partial(back_gather_kernel, nx),
        [cut, ((TILE, HID), F32)] + [node] * (nh - 1),
        [VMEM] * (nx + 1),
        add_over(total, "h", 1),
        *got,
    )
    back = self_back + last[0]
    if nh > 1:
        back = back + flip(last[1], "h", 1).astype(F32)
    grad_features = back.astype(BF)

    (whole,) = call(
        functools.partial(whole_kernel, w_rows),
        [wide],
        [SMEM] + [VMEM] * nx,
        where,
        total,
        *[shift(total, "x", d) for d in range(1, nx)],
    )
    across = flip(whole, "k", 1)
    first = jnp.where(k == 0, whole, across)
    second = jnp.where(k == 0, across, whole)[:HID]
    return hidden, grad_features, first[:HID], second, first[HID]


def on_mesh(mesh):
    row, col = ("h", "x", "k"), ("y", "l")
    nodes = P(row + col, None)
    in_specs = (
        nodes,
        P(row, col, None, None, None),
        P(row, col, None),
        P(row, col, None),
        P(row, col),
        P(row + col),
        P(),
        P(),
        P(),
        nodes,
    )
    out_specs = (nodes, nodes, P(), P(), P())
    return jax.shard_map(body, mesh=mesh, in_specs=in_specs, out_specs=out_specs, check_vma=False)


def solution(mesh):
    devices = mesh.devices.reshape(2, 4, 2, 8, 8)
    return on_mesh(Mesh(devices, ("h", "x", "k", "y", "l")))
```

```python
import functools

import jax
import jax.numpy as jnp
from jax import lax
from jax.experimental import pallas as pl
from jax.experimental.pallas import tpu as pltpu
from jax.sharding import Mesh, PartitionSpec as P

BF = jnp.bfloat16
F32 = jnp.float32
TILE = 128
HID = 256
QUAD = 4
CNT = 16
CHUNK = QUAD * TILE + CNT
VMEM = pl.BlockSpec(memory_space=pltpu.VMEM)
SMEM = pl.BlockSpec(memory_space=pltpu.SMEM)
PIECE = 80


def call(kernel, out, in_specs, *args, scratch=(), flops=0):
    shapes = [jax.ShapeDtypeStruct(s, t) for s, t in out]
    moved = sum(a.size * a.dtype.itemsize for a in args)
    moved += sum(s.size * s.dtype.itemsize for s in shapes)
    return pl.pallas_call(
        kernel,
        out_shape=shapes,
        in_specs=in_specs,
        out_specs=[VMEM] * len(shapes),
        scratch_shapes=list(scratch),
        compiler_params=pltpu.CompilerParams(vmem_limit_bytes=48 * 1024 * 1024),
        cost_estimate=pl.CostEstimate(flops=flops, bytes_accessed=moved, transcendentals=0),
    )(*args)


def split_counts(n):
    hi = n.astype(BF)
    lo = (n - hi.astype(F32)).astype(BF)
    return jnp.concatenate([hi, lo], axis=1)


def joined(block):
    return block[:, :TILE].astype(F32) + block[:, TILE:].astype(F32)


def row_counts(tile):
    ones = jnp.ones((8, TILE), BF)
    return lax.dot_general(ones, tile, (((1,), (1,)), ((), ())), preferred_element_type=F32)[0:1]


def add_counts(acc, chunk, lay, row):
    at = pl.multiple_of(chunk * CHUNK + QUAD * TILE, 16)
    mine = lax.broadcasted_iota(jnp.int32, (8, TILE), 0) == lay
    acc[pl.ds(at, 8), 0:TILE] += jnp.where(mine, jnp.broadcast_to(row, (8, TILE)), 0.0)


def contrib_kernel(slots, src, tiles, panel, msg, tiles_bf):
    rows = []
    for s in range(slots):
        tile = tiles[s].astype(F32).astype(BF)
        tiles_bf[s] = tile
        at = pl.multiple_of(src[s] * TILE, TILE)
        got = jnp.dot(tile, panel[pl.ds(at, TILE), :], preferred_element_type=F32)
        msg[s * TILE : (s + 1) * TILE, :] = got.astype(BF)
        rows.append(row_counts(tile))
    rows.append(jnp.zeros((CNT - slots, TILE), F32))
    counts = jnp.concatenate(rows, axis=0)
    msg[slots * TILE :, :] = jnp.concatenate([counts, jnp.zeros_like(counts)], axis=1).astype(BF)


def merge_kernel(slots, chunks, src, idx, other_idx, tiles, panel, recv, *refs):
    outs, acc = refs[:-1], refs[-1]
    acc[...] = jnp.zeros_like(acc)
    counts = recv[slots * TILE :, 0:TILE].astype(F32)

    def put(at, tile, row):
        chunk = at // QUAD
        lay = at % QUAD
        to = pl.multiple_of(chunk * CHUNK + lay * TILE, 16)
        acc[pl.ds(to, TILE), :] += tile
        add_counts(acc, chunk, lay, row)

    for s in range(slots):

        @pl.when(idx[s] >= 0)
        def _():
            at = pl.multiple_of(src[s] * TILE, TILE)
            got = jnp.dot(tiles[s], panel[pl.ds(at, TILE), :], preferred_element_type=F32)
            put(idx[s], got, row_counts(tiles[s]))

        @pl.when(other_idx[s] >= 0)
        def _():
            put(
                other_idx[s], recv[s * TILE : (s + 1) * TILE, :].astype(F32), counts[s : s + 1]
            )

    for o in range(chunks):
        at = o * CHUNK
        outs[o][0 : QUAD * TILE, :] = acc[at : at + QUAD * TILE, :].astype(BF)
        outs[o][QUAD * TILE :, :] = split_counts(acc[at + QUAD * TILE : at + CHUNK, 0:TILE])


def add_kernel(recv, own, out):
    n = QUAD * TILE
    out[0:n, :] = (recv[0:n, :].astype(F32) + own[0:n, :].astype(F32)).astype(BF)
    out[n:, :] = split_counts(joined(recv[n:, :]) + joined(own[n:, :]))


def ring_end_kernel(*refs):
    parts, keep, send = refs[:-2], refs[-2], refs[-1]
    half, n = 2 * TILE, QUAD * TILE
    first = sum(p[0:half, :].astype(F32) for p in parts)
    second = sum(p[half:n, :].astype(F32) for p in parts)
    counts = sum(joined(p[n:, :]) for p in parts)
    keep[0:half, :] = first
    keep[half:, :] = jnp.concatenate([counts, counts], axis=1)
    send[0:half, :] = second.astype(BF)
    send[half:, :] = split_counts(counts)


def half_kernel(keep_in, recv, keep, send):
    half = 2 * TILE
    counts = keep_in[half : half + 8, 0:TILE] + joined(recv[half:, :])[2:10]
    counts = jnp.concatenate([counts, counts], axis=0)
    keep[0:TILE, :] = keep_in[0:TILE, :] + recv[0:TILE, :].astype(F32)
    keep[TILE:, :] = jnp.concatenate([counts, counts], axis=1)
    send[0:TILE, :] = (keep_in[TILE:half, :] + recv[TILE:half, :].astype(F32)).astype(BF)
    send[TILE:, :] = split_counts(counts)


def degree_column(row):
    eye = lax.broadcasted_iota(jnp.int32, (TILE, TILE), 0) == lax.broadcasted_iota(
        jnp.int32, (TILE, TILE), 1
    )
    wide = jnp.broadcast_to(row, (TILE, TILE))
    return jnp.sum(jnp.where(eye, wide, 0.0), axis=1, keepdims=True)


def node_kernel(
    keep, recv, in_degree, features, w_self, w_neigh, bias, grad_out,
    hidden, aggregate, grad_pre, scaled,
):
    neigh = keep[0:TILE, :] + recv[0:TILE, :].astype(F32)
    edges = keep[TILE : TILE + 1, 0:TILE] + joined(recv[TILE:, :])[1:2]
    degree = degree_column(edges + in_degree[...].astype(F32))
    mean = (neigh / degree).astype(BF)
    aggregate[...] = mean
    v = (
        jnp.dot(features[...], w_self[...], preferred_element_type=F32)
        + jnp.dot(mean, w_neigh[...], preferred_element_type=F32)
        + bias[...]
    )
    c = 0.7978845608028654
    t = jnp.tanh(c * (v + 0.044715 * v * v * v))
    hidden[...] = (0.5 * v * (1.0 + t)).astype(BF)
    slope = 0.5 * (1.0 + t) + 0.5 * v * (1.0 - t * t) * (c * (1.0 + 3.0 * 0.044715 * v * v))
    g = (grad_out[...].astype(F32) * slope).astype(BF)
    grad_pre[...] = g
    back = lax.dot_general(g, w_neigh[...], (((1,), (1,)), ((), ())), preferred_element_type=F32)
    scaled[...] = (back / degree).astype(BF)


def weight_kernel(place, features, aggregate, grad_pre, w_self, keep, send, self_back):
    g = grad_pre[...]
    contract = (((0,), (0,)), ((), ()))
    first = lax.dot_general(features[...], g, contract, preferred_element_type=F32)
    second = lax.dot_general(aggregate[...], g, contract, preferred_element_type=F32)
    bias = jnp.broadcast_to(jnp.sum(g.astype(F32), axis=0, keepdims=True), (8, HID))
    mine = place[0] == 0
    keep[0:HID, :] = jnp.where(mine, first, second)
    send[0:HID, :] = jnp.where(mine, second, first)
    keep[HID:, :] = bias
    send[HID:, :] = bias
    self_back[...] = lax.dot_general(
        g, w_self[...], (((1,), (1,)), ((), ())), preferred_element_type=F32
    )


def weight_cut_kernel(size, place, keep_in, recv, *outs):
    rows = HID // size
    bias = keep_in[HID:, :] + recv[HID:, :]
    for d, ref in enumerate(outs):
        at = pl.multiple_of(lax.rem(place[1] + d, size) * rows, 8)
        block = keep_in[pl.ds(at, rows), :] + recv[pl.ds(at, rows), :]
        ref[...] = jnp.concatenate([block, bias, jnp.zeros_like(bias)], axis=0).astype(ref.dtype)


def pack_kernel(scaled, *refs):
    cuts, out = refs[:-1], refs[-1]
    out[0:TILE, :] = scaled[...]
    out[TILE:, :] = sum(c[...].astype(F32) for c in cuts).astype(BF)


def two_terms(value):
    hi = value.astype(BF)
    return jnp.concatenate([hi, (value - hi.astype(F32)).astype(BF)], axis=0)


def one_value(terms):
    return terms[0:PIECE].astype(F32) + terms[PIECE:].astype(F32)


def join_kernel(own, recv, out):
    n = own.shape[0] - PIECE
    out[0:n, :] = own[0:n, :]
    out[n : 2 * n, :] = recv[0:n, :]
    total = own[n:, :].astype(F32) + recv[n:, :].astype(F32)
    out[2 * n :, :] = two_terms(total) if n == 2 * TILE else total.astype(BF)


def piece_kernel(own, recv, out):
    n = own.shape[0] - 2 * PIECE
    out[...] = (one_value(own[n:, :]) + one_value(recv[n:, :])).astype(BF)


def pick_kernel(slots, chunks, idx, place, *refs):
    blocks, msg, held = refs[:chunks], refs[chunks], refs[chunks + 1]
    for s in range(slots):
        for o in range(chunks):

            @pl.when((idx[s] >= 0) & (idx[s] // QUAD == o))
            def _():
                at = pl.multiple_of((idx[s] % QUAD) * TILE, TILE)
                msg[s * TILE : (s + 1) * TILE, :] = blocks[o][pl.ds(at, TILE), :]

        @pl.when(idx[s] < 0)
        def _():
            msg[s * TILE : (s + 1) * TILE, :] = jnp.zeros((TILE, HID), BF)

    for o in range(chunks):
        held[lax.rem(place[2] + o, chunks)] = one_value(blocks[o][QUAD * TILE :, :])
    msg[slots * TILE :, :] = two_terms(sum(held[o] for o in range(chunks)))


def back_kernel(slots, chunks, src, idx, live, tiles, recv, *refs):
    blocks, (keep, send, acc, got) = refs[:chunks], refs[chunks:]
    acc[...] = jnp.zeros_like(acc)
    for s in range(slots):

        @pl.when(live[s] > 0)
        def _():
            for o in range(chunks):

                @pl.when((idx[s] >= 0) & (idx[s] // QUAD == o))
                def _():
                    at = pl.multiple_of((idx[s] % QUAD) * TILE, TILE)
                    got[...] = blocks[o][pl.ds(at, TILE), :]

            @pl.when(idx[s] < 0)
            def _():
                got[...] = recv[s * TILE : (s + 1) * TILE, :]

            term = lax.dot_general(
                tiles[s], got[...], (((0,), (0,)), ((), ())), preferred_element_type=F32
            )
            to = pl.multiple_of(src[s] * TILE, TILE)
            acc[pl.ds(to, TILE), :] += term

    half = keep.shape[0]
    keep[...] = acc[0:half, :]
    send[...] = acc[half:, :].astype(BF)


def back_cut_kernel(keep_in, recv, piece_in, far_piece, keep, piece, *sends):
    piece[...] = (piece_in[...].astype(F32) + far_piece[...].astype(F32)).astype(BF)
    rows = keep.shape[0]
    for d, ref in enumerate((keep,) + sends):
        at = d * rows
        got = keep_in[at : at + rows, :] + recv[at : at + rows, :].astype(F32)
        ref[0:rows, :] = got.astype(ref.dtype)
        if d:
            ref[rows:, :] = piece[...]


def back_gather_kernel(size, place, near, piece, *refs):
    recvs, (whole, *outs) = refs[: size - 1], refs[size - 1 :]
    rows, n = HID // size, near.shape[0]
    for d, ref in enumerate(outs):
        at = slice(d * TILE, (d + 1) * TILE)
        ref[...] = (near[at, :] + sum(r[at, :].astype(F32) for r in recvs)).astype(ref.dtype)
    for d in range(size):
        at = lax.rem(place[1] + size - d, size)
        block = piece[...] if d == 0 else recvs[d - 1][n:, :]
        whole[pl.ds(pl.multiple_of(at * rows, 16), rows), :] = block[0:rows, :]

        @pl.when(at == 0)
        def _():
            whole[HID:, :] = block[rows:, :]


def body(
    features,
    tile_values,
    tile_block_row,
    tile_block_col,
    tile_count,
    in_degree,
    w_self,
    w_neigh,
    bias,
    grad_out,
):
    nh, nx, nk, ny, nl = (lax.axis_size(a) for a in ("h", "x", "k", "y", "l"))
    h, x, k, y, l = (lax.axis_index(a) for a in ("h", "x", "k", "y", "l"))
    slots = tile_values.shape[2]
    sources = nh * nx * nk

    def flip(value, axis, bit):
        n = lax.axis_size(axis)
        return lax.ppermute(value, axis, [(i, i ^ bit) for i in range(n)])

    def shift(value, axis, by):
        n = lax.axis_size(axis)
        return lax.ppermute(value, axis, [(i, (i + by) % n) for i in range(n)])

    slot = jnp.arange(slots, dtype=jnp.int32)
    live = (slot < tile_count[0, 0]).astype(jnp.int32)
    dest = jnp.where(live > 0, tile_block_row[0, 0], -1)
    source = tile_block_col[0, 0]
    sh, sx, sk = source // (nx * nk), (source // nk) % nx, source % nk
    src = ((sk ^ k) * nx + (sx - x) % nx) * nh + (sh ^ h)

    def place(d):
        dl = d % nl
        far = (dl >> 1) ^ (l >> 1)
        lay = ((far & 1) << 1) | (far >> 1)
        mine = (d >= 0) & ((dl & 1) == (l & 1))
        return jnp.where(mine, ((d // nl - y) % ny) * QUAD + lay, -1)

    meta = jnp.zeros((8, TILE), jnp.int32).at[0, :slots].set(dest)
    other = flip(meta, "l", 1)[0, :slots]
    own_idx, other_idx = place(dest), place(other)
    where = jnp.stack([k, x, y]).astype(jnp.int32)

    panel = features
    if nh > 1:
        panel = jnp.concatenate([panel, flip(panel, "h", 1)], axis=0)
    panel = jnp.concatenate([panel] + [shift(panel, "x", -d) for d in range(1, nx)], axis=0)
    panel = jnp.concatenate([panel, flip(panel, "k", 1)], axis=0)

    tile_flops = 2 * slots * TILE * TILE * HID
    msg, tiles = call(
        functools.partial(contrib_kernel, slots),
        [((slots * TILE + CNT, HID), BF), ((slots, TILE, TILE), BF)],
        [SMEM, VMEM, VMEM],
        src,
        tile_values[0, 0],
        panel,
        flops=tile_flops,
    )
    chunks = call(
        functools.partial(merge_kernel, slots, ny),
        [((CHUNK, HID), BF)] * ny,
        [SMEM, SMEM, SMEM, VMEM, VMEM, VMEM],
        src,
        own_idx,
        other_idx,
        tiles,
        panel,
        flip(msg, "l", 1),
        scratch=[pltpu.VMEM((ny * CHUNK, HID), F32)],
        flops=tile_flops,
    )

    ups, downs = ny // 2, ny - 1 - ny // 2
    up, down = chunks[ups], chunks[(-downs) % ny]
    parts = [chunks[0]]
    for step in range(1, ups + 1):
        up = shift(up, "y", 1)
        if step <= downs:
            down = shift(down, "y", -1)
        if step < ups:
            (up,) = call(add_kernel, [((CHUNK, HID), BF)], [VMEM] * 2, up, chunks[ups - step])
        if step < downs:
            (down,) = call(
                add_kernel, [((CHUNK, HID), BF)], [VMEM] * 2, down, chunks[ny - downs + step]
            )
    parts.append(up)
    if downs:
        parts.append(down)
    half_rows, last_rows = 2 * TILE + CNT, TILE + CNT
    keep, send = call(
        ring_end_kernel,
        [((half_rows, HID), F32), ((half_rows, HID), BF)],
        [VMEM] * len(parts),
        *parts,
    )
    keep, send = call(
        half_kernel,
        [((last_rows, HID), F32), ((last_rows, HID), BF)],
        [VMEM] * 2,
        keep,
        flip(send, "l", 2),
    )
    node = ((TILE, HID), BF)
    hidden, aggregate, grad_pre, scaled = call(
        node_kernel,
        [node] * 4,
        [VMEM] * 8,
        keep,
        flip(send, "l", 4),
        in_degree.reshape(1, TILE),
        features,
        w_self,
        w_neigh,
        bias.reshape(1, HID),
        grad_out,
        flops=6 * TILE * HID * HID,
    )

    wide = ((HID + 8, HID), F32)
    w_keep, w_send, self_back = call(
        weight_kernel,
        [wide, wide, ((TILE, HID), F32)],
        [SMEM] + [VMEM] * 4,
        where,
        features,
        aggregate,
        grad_pre,
        w_self,
        flops=6 * TILE * HID * HID,
    )
    cuts = call(
        functools.partial(weight_cut_kernel, nx),
        [((PIECE, HID), F32)] + [((PIECE, HID), BF)] * (nx - 1),
        [SMEM, VMEM, VMEM],
        where,
        w_keep,
        flip(w_send, "k", 1),
    )
    cuts = [cuts[0]] + [shift(cuts[d], "x", d) for d in range(1, nx)]

    (packed,) = call(
        pack_kernel, [((TILE + PIECE, HID), BF)], [VMEM] * (nx + 1), scaled, *cuts
    )
    for bit, rows in ((4, 2 * TILE + PIECE), (2, 4 * TILE + 2 * PIECE)):
        (packed,) = call(
            join_kernel,
            [((rows, HID), BF)],
            [VMEM] * 2,
            packed,
            flip(packed, "l", bit),
        )
    blocks = [packed] * ny
    up = down = packed
    for step in range(1, ups + 1):
        up = shift(up, "y", 1)
        blocks[(-step) % ny] = up
        if step <= downs:
            down = shift(down, "y", -1)
            blocks[step] = down
    (msg,) = call(
        functools.partial(pick_kernel, slots, ny),
        [((slots * TILE + 2 * PIECE, HID), BF)],
        [SMEM, SMEM] + [VMEM] * ny,
        other_idx,
        where,
        *blocks,
        scratch=[pltpu.VMEM((ny, PIECE, HID), F32)],
    )
    got = flip(msg, "l", 1)
    (piece,) = call(piece_kernel, [((PIECE, HID), BF)], [VMEM] * 2, msg, got)
    far_piece = flip(piece, "h", 1) if nh > 1 else jnp.zeros_like(piece)

    half = sources // 2 * TILE
    keep, send = call(
        functools.partial(back_kernel, slots, ny),
        [((half, HID), F32), ((half, HID), BF)],
        [SMEM, SMEM, SMEM, VMEM, VMEM] + [VMEM] * ny,
        src,
        own_idx,
        live,
        tiles,
        got,
        *blocks,
        scratch=[pltpu.VMEM((sources * TILE, HID), F32), pltpu.VMEM((TILE, HID), BF)],
        flops=tile_flops,
    )
    group = nh * TILE
    near, piece, *sends = call(
        back_cut_kernel,
        [((group, HID), F32), ((PIECE, HID), BF)] + [((group + PIECE, HID), BF)] * (nx - 1),
        [VMEM] * 4,
        keep,
        flip(send, "k", 1),
        piece,
        far_piece,
    )
    whole, *last = call(
        functools.partial(back_gather_kernel, nx),
        [((HID + 16, HID), BF), ((TILE, HID), F32)] + [node] * (nh - 1),
        [SMEM] + [VMEM] * (nx + 1),
        where,
        near,
        piece,
        *[shift(sends[d - 1], "x", d) for d in range(1, nx)],
    )
    back = self_back + last[0]
    if nh > 1:
        back = back + flip(last[1], "h", 1).astype(F32)
    grad_features = back.astype(BF)
    across = flip(whole, "k", 1)
    first = jnp.where(k == 0, whole, across).astype(F32)
    second = jnp.where(k == 0, across, whole)[:HID].astype(F32)
    return hidden, grad_features, first[:HID], second, first[HID]


def on_mesh(mesh):
    row, col = ("h", "x", "k"), ("y", "l")
    nodes = P(row + col, None)
    in_specs = (
        nodes,
        P(row, col, None, None, None),
        P(row, col, None),
        P(row, col, None),
        P(row, col),
        P(row + col),
        P(),
        P(),
        P(),
        nodes,
    )
    out_specs = (nodes, nodes, P(), P(), P())
    return jax.shard_map(body, mesh=mesh, in_specs=in_specs, out_specs=out_specs, check_vma=False)


def solution(mesh):
    devices = mesh.devices.reshape(2, 4, 2, 8, 8)
    return on_mesh(Mesh(devices, ("h", "x", "k", "y", "l")))
```

```python
import functools

import jax
import jax.numpy as jnp
from jax import lax
from jax.experimental import pallas as pl
from jax.experimental.pallas import tpu as pltpu
from jax.sharding import Mesh, PartitionSpec as P

BF = jnp.bfloat16
F32 = jnp.float32
TILE = 128
HID = 256
QUAD = 4
CNT = 16
CHUNK = QUAD * TILE + CNT
VMEM = pl.BlockSpec(memory_space=pltpu.VMEM)
SMEM = pl.BlockSpec(memory_space=pltpu.SMEM)
AFTER = pl.BlockSpec(memory_space=pl.ANY)
PIECE = 80


def call(kernel, out, in_specs, *args, scratch=(), flops=0):
    shapes = [jax.ShapeDtypeStruct(s, t) for s, t in out]
    moved = sum(a.size * a.dtype.itemsize for a in args)
    moved += sum(s.size * s.dtype.itemsize for s in shapes)
    return pl.pallas_call(
        kernel,
        out_shape=shapes,
        in_specs=in_specs,
        out_specs=[VMEM] * len(shapes),
        scratch_shapes=list(scratch),
        compiler_params=pltpu.CompilerParams(vmem_limit_bytes=48 * 1024 * 1024),
        cost_estimate=pl.CostEstimate(flops=flops, bytes_accessed=moved, transcendentals=0),
    )(*args)


def split_counts(n):
    hi = n.astype(BF)
    lo = (n - hi.astype(F32)).astype(BF)
    return jnp.concatenate([hi, lo], axis=1)


def joined(block):
    return block[:, :TILE].astype(F32) + block[:, TILE:].astype(F32)


def row_counts(tile):
    ones = jnp.ones((8, TILE), BF)
    return lax.dot_general(ones, tile, (((1,), (1,)), ((), ())), preferred_element_type=F32)[0:1]


def add_counts(acc, chunk, lay, row):
    at = pl.multiple_of(chunk * CHUNK + QUAD * TILE, 16)
    mine = lax.broadcasted_iota(jnp.int32, (8, TILE), 0) == lay
    acc[pl.ds(at, 8), 0:TILE] += jnp.where(mine, jnp.broadcast_to(row, (8, TILE)), 0.0)


def contrib_kernel(slots, src, tiles, panel, msg, tiles_bf):
    rows = []
    for s in range(slots):
        tile = tiles[s].astype(F32).astype(BF)
        tiles_bf[s] = tile
        at = pl.multiple_of(src[s] * TILE, TILE)
        got = jnp.dot(tile, panel[pl.ds(at, TILE), :], preferred_element_type=F32)
        msg[s * TILE : (s + 1) * TILE, :] = got.astype(BF)
        rows.append(row_counts(tile))
    rows.append(jnp.zeros((CNT - slots, TILE), F32))
    counts = jnp.concatenate(rows, axis=0)
    msg[slots * TILE :, :] = jnp.concatenate([counts, jnp.zeros_like(counts)], axis=1).astype(BF)


def merge_kernel(slots, chunks, src, idx, other_idx, tiles, panel, recv, *refs):
    outs, acc = refs[:-1], refs[-1]
    acc[...] = jnp.zeros_like(acc)
    counts = recv[slots * TILE :, 0:TILE].astype(F32)

    def put(at, tile, row):
        chunk = at // QUAD
        lay = at % QUAD
        to = pl.multiple_of(chunk * CHUNK + lay * TILE, 16)
        acc[pl.ds(to, TILE), :] += tile
        add_counts(acc, chunk, lay, row)

    for s in range(slots):

        @pl.when(idx[s] >= 0)
        def _():
            at = pl.multiple_of(src[s] * TILE, TILE)
            got = jnp.dot(tiles[s], panel[pl.ds(at, TILE), :], preferred_element_type=F32)
            put(idx[s], got, row_counts(tiles[s]))

        @pl.when(other_idx[s] >= 0)
        def _():
            put(
                other_idx[s], recv[s * TILE : (s + 1) * TILE, :].astype(F32), counts[s : s + 1]
            )

    for o in range(chunks):
        at = o * CHUNK
        outs[o][0 : QUAD * TILE, :] = acc[at : at + QUAD * TILE, :].astype(BF)
        outs[o][QUAD * TILE :, :] = split_counts(acc[at + QUAD * TILE : at + CHUNK, 0:TILE])


def add_kernel(recv, own, out):
    n = QUAD * TILE
    out[0:n, :] = (recv[0:n, :].astype(F32) + own[0:n, :].astype(F32)).astype(BF)
    out[n:, :] = split_counts(joined(recv[n:, :]) + joined(own[n:, :]))


def ring_end_kernel(*refs):
    parts, keep, send = refs[:-2], refs[-2], refs[-1]
    half, n = 2 * TILE, QUAD * TILE
    first = sum(p[0:half, :].astype(F32) for p in parts)
    second = sum(p[half:n, :].astype(F32) for p in parts)
    counts = sum(joined(p[n:, :]) for p in parts)
    keep[0:half, :] = first
    keep[half:, :] = jnp.concatenate([counts, counts], axis=1)
    send[0:half, :] = second.astype(BF)
    send[half:, :] = split_counts(counts)


def half_kernel(keep_in, recv, keep, send):
    half = 2 * TILE
    counts = keep_in[half : half + 8, 0:TILE] + joined(recv[half:, :])[2:10]
    counts = jnp.concatenate([counts, counts], axis=0)
    keep[0:TILE, :] = keep_in[0:TILE, :] + recv[0:TILE, :].astype(F32)
    keep[TILE:, :] = jnp.concatenate([counts, counts], axis=1)
    send[0:TILE, :] = (keep_in[TILE:half, :] + recv[TILE:half, :].astype(F32)).astype(BF)
    send[TILE:, :] = split_counts(counts)


def degree_column(row):
    eye = lax.broadcasted_iota(jnp.int32, (TILE, TILE), 0) == lax.broadcasted_iota(
        jnp.int32, (TILE, TILE), 1
    )
    wide = jnp.broadcast_to(row, (TILE, TILE))
    return jnp.sum(jnp.where(eye, wide, 0.0), axis=1, keepdims=True)


def node_kernel(
    keep, recv, in_degree, features, w_self, w_neigh, bias, grad_out,
    hidden, aggregate, grad_pre, scaled,
):
    neigh = keep[0:TILE, :] + recv[0:TILE, :].astype(F32)
    edges = keep[TILE : TILE + 1, 0:TILE] + joined(recv[TILE:, :])[1:2]
    degree = degree_column(edges + in_degree[...].astype(F32))
    mean = (neigh / degree).astype(BF)
    aggregate[...] = mean
    v = (
        jnp.dot(features[...], w_self[...], preferred_element_type=F32)
        + jnp.dot(mean, w_neigh[...], preferred_element_type=F32)
        + bias[...]
    )
    c = 0.7978845608028654
    t = jnp.tanh(c * (v + 0.044715 * v * v * v))
    hidden[...] = (0.5 * v * (1.0 + t)).astype(BF)
    slope = 0.5 * (1.0 + t) + 0.5 * v * (1.0 - t * t) * (c * (1.0 + 3.0 * 0.044715 * v * v))
    g = (grad_out[...].astype(F32) * slope).astype(BF)
    grad_pre[...] = g
    back = lax.dot_general(g, w_neigh[...], (((1,), (1,)), ((), ())), preferred_element_type=F32)
    scaled[...] = (back / degree).astype(BF)


def weight_kernel(size, features, aggregate, grad_pre, w_self, cuts, self_back):
    g = grad_pre[...]
    contract = (((0,), (0,)), ((), ()))
    first = lax.dot_general(features[...], g, contract, preferred_element_type=F32)
    second = lax.dot_general(aggregate[...], g, contract, preferred_element_type=F32)
    bias = jnp.broadcast_to(jnp.sum(g.astype(F32), axis=0, keepdims=True), (PIECE - 64, HID))
    rows = HID // size
    for i in range(size):
        for j, terms in enumerate((first, second)):
            at = (i * 2 + j) * PIECE
            cuts[at : at + rows, :] = terms[i * rows : (i + 1) * rows].astype(BF)
            cuts[at + rows : at + PIECE, :] = bias[0 : PIECE - rows].astype(BF)
    self_back[...] = lax.dot_general(
        g, w_self[...], (((1,), (1,)), ((), ())), preferred_element_type=F32
    )


def pack_kernel(scaled, cuts, out):
    out[0:TILE, :] = scaled[...]
    pieces = [cuts[i : i + PIECE, :].astype(F32) for i in range(0, cuts.shape[0], PIECE)]
    out[TILE:, :] = sum(pieces).astype(BF)


def two_terms(value):
    hi = value.astype(BF)
    return jnp.concatenate([hi, (value - hi.astype(F32)).astype(BF)], axis=0)


def one_value(terms):
    return terms[0:PIECE].astype(F32) + terms[PIECE:].astype(F32)


def join_kernel(own, recv, out):
    n = own.shape[0] - PIECE
    out[0:n, :] = own[0:n, :]
    out[n : 2 * n, :] = recv[0:n, :]
    total = own[n:, :].astype(F32) + recv[n:, :].astype(F32)
    out[2 * n :, :] = two_terms(total) if n == 2 * TILE else total.astype(BF)


def twin_kernel(own, recv, out):
    out[...] = two_terms(own[...].astype(F32) + recv[...].astype(F32))


def pick_kernel(slots, chunks, idx, place, *refs):
    blocks, (msg, piece, held) = refs[:chunks], refs[chunks:]
    for s in range(slots):
        for o in range(chunks):

            @pl.when((idx[s] >= 0) & (idx[s] // QUAD == o))
            def _():
                at = pl.multiple_of((idx[s] % QUAD) * TILE, TILE)
                msg[s * TILE : (s + 1) * TILE, :] = blocks[o][pl.ds(at, TILE), :]

        @pl.when(idx[s] < 0)
        def _():
            msg[s * TILE : (s + 1) * TILE, :] = jnp.zeros((TILE, HID), BF)

    for o in range(chunks):
        held[lax.rem(place[2] + o, chunks)] = one_value(blocks[o][QUAD * TILE :, :])
    piece[...] = sum(held[o] for o in range(chunks)).astype(BF)


def back_kernel(slots, chunks, src, idx, live, tiles, recv, after, *refs):
    blocks, (keep, send, acc, got) = refs[:chunks], refs[chunks:]
    acc[...] = jnp.zeros_like(acc)
    for s in range(slots):

        @pl.when(live[s] > 0)
        def _():
            for o in range(chunks):

                @pl.when((idx[s] >= 0) & (idx[s] // QUAD == o))
                def _():
                    at = pl.multiple_of((idx[s] % QUAD) * TILE, TILE)
                    got[...] = blocks[o][pl.ds(at, TILE), :]

            @pl.when(idx[s] < 0)
            def _():
                got[...] = recv[s * TILE : (s + 1) * TILE, :]

            term = lax.dot_general(
                tiles[s], got[...], (((0,), (0,)), ((), ())), preferred_element_type=F32
            )
            to = pl.multiple_of(src[s] * TILE, TILE)
            acc[pl.ds(to, TILE), :] += term

    half = keep.shape[0]
    keep[...] = acc[0:half, :]
    send[...] = acc[half:, :].astype(BF)


def back_cut_kernel(keep_in, recv, twin, other_twin, keep, piece, *sends):
    piece[...] = (one_value(twin[...]) + one_value(other_twin[...])).astype(BF)
    rows = keep.shape[0]
    for d, ref in enumerate((keep,) + sends):
        at = d * rows
        got = keep_in[at : at + rows, :] + recv[at : at + rows, :].astype(F32)
        ref[0:rows, :] = got.astype(ref.dtype)
        if d:
            ref[rows:, :] = piece[...]


def back_gather_kernel(size, place, near, piece, *refs):
    recvs, (whole, *outs) = refs[: size - 1], refs[size - 1 :]
    rows, n = HID // size, near.shape[0]
    for d, ref in enumerate(outs):
        at = slice(d * TILE, (d + 1) * TILE)
        ref[...] = (near[at, :] + sum(r[at, :].astype(F32) for r in recvs)).astype(ref.dtype)
    for d in range(size):
        at = lax.rem(place[1] + size - d, size)
        block = piece[...] if d == 0 else recvs[d - 1][n:, :]
        whole[pl.ds(pl.multiple_of(at * rows, 16), rows), :] = block[0:rows, :]

        @pl.when(at == 0)
        def _():
            whole[HID:, :] = block[rows:, :]


def last_kernel(place, self_back, near, far, whole, across, grads, first, second, bias):
    grads[...] = (self_back[...] + near[...] + far[...].astype(F32)).astype(BF)
    mine, other = whole[...].astype(F32), across[...].astype(F32)
    own = place[0] == 0
    first[...] = jnp.where(own, mine[0:HID], other[0:HID])
    second[...] = jnp.where(own, other[0:HID], mine[0:HID])
    bias[...] = jnp.where(own, mine[HID : HID + 1], other[HID : HID + 1])


def body(
    features,
    tile_values,
    tile_block_row,
    tile_block_col,
    tile_count,
    in_degree,
    w_self,
    w_neigh,
    bias,
    grad_out,
):
    nh, nx, nk, ny, nl = (lax.axis_size(a) for a in ("h", "x", "k", "y", "l"))
    h, x, k, y, l = (lax.axis_index(a) for a in ("h", "x", "k", "y", "l"))
    slots = tile_values.shape[2]
    sources = nh * nx * nk

    def flip(value, axis, bit):
        n = lax.axis_size(axis)
        return lax.ppermute(value, axis, [(i, i ^ bit) for i in range(n)])

    def shift(value, axis, by):
        n = lax.axis_size(axis)
        return lax.ppermute(value, axis, [(i, (i + by) % n) for i in range(n)])

    slot = jnp.arange(slots, dtype=jnp.int32)
    live = (slot < tile_count[0, 0]).astype(jnp.int32)
    dest = jnp.where(live > 0, tile_block_row[0, 0], -1)
    source = tile_block_col[0, 0]
    sh, sx, sk = source // (nx * nk), (source // nk) % nx, source % nk
    src = ((sk ^ k) * nx + (sx - x) % nx) * nh + (sh ^ h)

    def place(d):
        dl = d % nl
        far = (dl >> 1) ^ (l >> 1)
        lay = ((far & 1) << 1) | (far >> 1)
        mine = (d >= 0) & ((dl & 1) == (l & 1))
        return jnp.where(mine, ((d // nl - y) % ny) * QUAD + lay, -1)

    meta = jnp.zeros((8, TILE), jnp.int32).at[0, :slots].set(dest)
    other = flip(meta, "l", 1)[0, :slots]
    own_idx, other_idx = place(dest), place(other)
    where = jnp.stack([k, x, y]).astype(jnp.int32)

    panel = features
    if nh > 1:
        panel = jnp.concatenate([panel, flip(panel, "h", 1)], axis=0)
    panel = jnp.concatenate([panel] + [shift(panel, "x", -d) for d in range(1, nx)], axis=0)
    panel = jnp.concatenate([panel, flip(panel, "k", 1)], axis=0)

    tile_flops = 2 * slots * TILE * TILE * HID
    msg, tiles = call(
        functools.partial(contrib_kernel, slots),
        [((slots * TILE + CNT, HID), BF), ((slots, TILE, TILE), BF)],
        [SMEM, VMEM, VMEM],
        src,
        tile_values[0, 0],
        panel,
        flops=tile_flops,
    )
    chunks = call(
        functools.partial(merge_kernel, slots, ny),
        [((CHUNK, HID), BF)] * ny,
        [SMEM, SMEM, SMEM, VMEM, VMEM, VMEM],
        src,
        own_idx,
        other_idx,
        tiles,
        panel,
        flip(msg, "l", 1),
        scratch=[pltpu.VMEM((ny * CHUNK, HID), F32)],
        flops=tile_flops,
    )

    ups, downs = ny // 2, ny - 1 - ny // 2
    up, down = chunks[ups], chunks[(-downs) % ny]
    parts = [chunks[0]]
    for step in range(1, ups + 1):
        up = shift(up, "y", 1)
        if step <= downs:
            down = shift(down, "y", -1)
        if step < ups:
            (up,) = call(add_kernel, [((CHUNK, HID), BF)], [VMEM] * 2, up, chunks[ups - step])
        if step < downs:
            (down,) = call(
                add_kernel, [((CHUNK, HID), BF)], [VMEM] * 2, down, chunks[ny - downs + step]
            )
    parts.append(up)
    if downs:
        parts.append(down)
    half_rows, last_rows = 2 * TILE + CNT, TILE + CNT
    keep, send = call(
        ring_end_kernel,
        [((half_rows, HID), F32), ((half_rows, HID), BF)],
        [VMEM] * len(parts),
        *parts,
    )
    keep, send = call(
        half_kernel,
        [((last_rows, HID), F32), ((last_rows, HID), BF)],
        [VMEM] * 2,
        keep,
        flip(send, "l", 2),
    )
    node = ((TILE, HID), BF)
    hidden, aggregate, grad_pre, scaled = call(
        node_kernel,
        [node] * 4,
        [VMEM] * 8,
        keep,
        flip(send, "l", 4),
        in_degree.reshape(1, TILE),
        features,
        w_self,
        w_neigh,
        bias.reshape(1, HID),
        grad_out,
        flops=6 * TILE * HID * HID,
    )

    cuts, self_back = call(
        functools.partial(weight_kernel, nx),
        [((nx * nk * PIECE, HID), BF), ((TILE, HID), F32)],
        [VMEM] * 4,
        features,
        aggregate,
        grad_pre,
        w_self,
        flops=6 * TILE * HID * HID,
    )
    cuts = lax.all_to_all(cuts, ("x", "k"), split_axis=0, concat_axis=0, tiled=True)

    (packed,) = call(pack_kernel, [((TILE + PIECE, HID), BF)], [VMEM] * 2, scaled, cuts)
    for bit, rows in ((4, 2 * TILE + PIECE), (2, 4 * TILE + 2 * PIECE)):
        (packed,) = call(
            join_kernel,
            [((rows, HID), BF)],
            [VMEM] * 2,
            packed,
            flip(packed, "l", bit),
        )
    blocks = [packed] * ny
    up = down = packed
    for step in range(1, ups + 1):
        up = shift(up, "y", 1)
        blocks[(-step) % ny] = up
        if step <= downs:
            down = shift(down, "y", -1)
            blocks[step] = down
    msg, piece = call(
        functools.partial(pick_kernel, slots, ny),
        [((slots * TILE, HID), BF), ((PIECE, HID), BF)],
        [SMEM, SMEM] + [VMEM] * ny,
        other_idx,
        where,
        *blocks,
        scratch=[pltpu.VMEM((ny, PIECE, HID), F32)],
    )
    got = flip(msg, "l", 1)
    far_piece = flip(piece, "h", 1) if nh > 1 else jnp.zeros_like(piece)
    (twin,) = call(twin_kernel, [((2 * PIECE, HID), BF)], [VMEM] * 2, piece, far_piece)

    half = sources // 2 * TILE
    keep, send = call(
        functools.partial(back_kernel, slots, ny),
        [((half, HID), F32), ((half, HID), BF)],
        [SMEM, SMEM, SMEM, VMEM, VMEM, AFTER] + [VMEM] * ny,
        src,
        own_idx,
        live,
        tiles,
        got,
        twin,
        *blocks,
        scratch=[pltpu.VMEM((sources * TILE, HID), F32), pltpu.VMEM((TILE, HID), BF)],
        flops=tile_flops,
    )
    group = nh * TILE
    near, piece, *sends = call(
        back_cut_kernel,
        [((group, HID), F32), ((PIECE, HID), BF)] + [((group + PIECE, HID), BF)] * (nx - 1),
        [VMEM] * 4,
        keep,
        flip(send, "k", 1),
        twin,
        flip(twin, "l", 1),
    )
    whole, *last = call(
        functools.partial(back_gather_kernel, nx),
        [((HID + 16, HID), BF), ((TILE, HID), F32)] + [node] * (nh - 1),
        [SMEM] + [VMEM] * (nx + 1),
        where,
        near,
        piece,
        *[shift(sends[d - 1], "x", d) for d in range(1, nx)],
    )
    far = flip(last[1], "h", 1) if nh > 1 else jnp.zeros((TILE, HID), BF)
    grad_features, grad_w_self, grad_w_neigh, grad_bias = call(
        last_kernel,
        [node, ((HID, HID), F32), ((HID, HID), F32), ((1, HID), F32)],
        [SMEM] + [VMEM] * 5,
        where,
        self_back,
        last[0],
        far,
        whole,
        flip(whole, "k", 1),
    )
    return hidden, grad_features, grad_w_self, grad_w_neigh, grad_bias.reshape(HID)


def on_mesh(mesh):
    row, col = ("h", "x", "k"), ("y", "l")
    nodes = P(row + col, None)
    in_specs = (
        nodes,
        P(row, col, None, None, None),
        P(row, col, None),
        P(row, col, None),
        P(row, col),
        P(row + col),
        P(),
        P(),
        P(),
        nodes,
    )
    out_specs = (nodes, nodes, P(), P(), P())
    return jax.shard_map(body, mesh=mesh, in_specs=in_specs, out_specs=out_specs, check_vma=False)


def solution(mesh):
    devices = mesh.devices.reshape(2, 4, 2, 8, 8)
    return on_mesh(Mesh(devices, ("h", "x", "k", "y", "l")))
```

```python
import functools

import jax
import jax.numpy as jnp
from jax import lax
from jax.experimental import pallas as pl
from jax.experimental.pallas import tpu as pltpu
from jax.sharding import Mesh, PartitionSpec as P

BF = jnp.bfloat16
F32 = jnp.float32
TILE = 128
HID = 256
QUAD = 4
CNT = 16
CHUNK = QUAD * TILE + CNT
VMEM = pl.BlockSpec(memory_space=pltpu.VMEM)
SMEM = pl.BlockSpec(memory_space=pltpu.SMEM)
PIECE = 80


def call(kernel, out, in_specs, *args, scratch=(), flops=0):
    shapes = [jax.ShapeDtypeStruct(s, t) for s, t in out]
    moved = sum(a.size * a.dtype.itemsize for a in args)
    moved += sum(s.size * s.dtype.itemsize for s in shapes)
    return pl.pallas_call(
        kernel,
        out_shape=shapes,
        in_specs=in_specs,
        out_specs=[VMEM] * len(shapes),
        scratch_shapes=list(scratch),
        compiler_params=pltpu.CompilerParams(vmem_limit_bytes=48 * 1024 * 1024),
        cost_estimate=pl.CostEstimate(flops=flops, bytes_accessed=moved, transcendentals=0),
    )(*args)


def split_counts(n):
    hi = n.astype(BF)
    lo = (n - hi.astype(F32)).astype(BF)
    return jnp.concatenate([hi, lo], axis=1)


def joined(block):
    return block[:, :TILE].astype(F32) + block[:, TILE:].astype(F32)


def row_counts(tile):
    ones = jnp.ones((8, TILE), BF)
    return lax.dot_general(ones, tile, (((1,), (1,)), ((), ())), preferred_element_type=F32)[0:1]


def add_counts(acc, chunk, lay, row):
    at = pl.multiple_of(chunk * CHUNK + QUAD * TILE, 16)
    mine = lax.broadcasted_iota(jnp.int32, (8, TILE), 0) == lay
    acc[pl.ds(at, 8), 0:TILE] += jnp.where(mine, jnp.broadcast_to(row, (8, TILE)), 0.0)


def contrib_kernel(slots, src, tiles, panel, msg, tiles_bf):
    rows = []
    for s in range(slots):
        tile = tiles[s].astype(F32).astype(BF)
        tiles_bf[s] = tile
        at = pl.multiple_of(src[s] * TILE, TILE)
        got = jnp.dot(tile, panel[pl.ds(at, TILE), :], preferred_element_type=F32)
        msg[s * TILE : (s + 1) * TILE, :] = got.astype(BF)
        rows.append(row_counts(tile))
    rows.append(jnp.zeros((CNT - slots, TILE), F32))
    counts = jnp.concatenate(rows, axis=0)
    msg[slots * TILE :, :] = jnp.concatenate([counts, jnp.zeros_like(counts)], axis=1).astype(BF)


def merge_kernel(slots, chunks, src, idx, other_idx, tiles, panel, recv, *refs):
    outs, acc = refs[:-1], refs[-1]
    acc[...] = jnp.zeros_like(acc)
    counts = recv[slots * TILE :, 0:TILE].astype(F32)

    def put(at, tile, row):
        chunk = at // QUAD
        lay = at % QUAD
        to = pl.multiple_of(chunk * CHUNK + lay * TILE, 16)
        acc[pl.ds(to, TILE), :] += tile
        add_counts(acc, chunk, lay, row)

    for s in range(slots):

        @pl.when(idx[s] >= 0)
        def _():
            at = pl.multiple_of(src[s] * TILE, TILE)
            got = jnp.dot(tiles[s], panel[pl.ds(at, TILE), :], preferred_element_type=F32)
            put(idx[s], got, row_counts(tiles[s]))

        @pl.when(other_idx[s] >= 0)
        def _():
            put(
                other_idx[s], recv[s * TILE : (s + 1) * TILE, :].astype(F32), counts[s : s + 1]
            )

    for o in range(chunks):
        at = o * CHUNK
        outs[o][0 : QUAD * TILE, :] = acc[at : at + QUAD * TILE, :].astype(BF)
        outs[o][QUAD * TILE :, :] = split_counts(acc[at + QUAD * TILE : at + CHUNK, 0:TILE])


def add_kernel(recv, own, out):
    n = QUAD * TILE
    out[0:n, :] = (recv[0:n, :].astype(F32) + own[0:n, :].astype(F32)).astype(BF)
    out[n:, :] = split_counts(joined(recv[n:, :]) + joined(own[n:, :]))


def ring_end_kernel(*refs):
    parts, keep, send = refs[:-2], refs[-2], refs[-1]
    half, n = 2 * TILE, QUAD * TILE
    first = sum(p[0:half, :].astype(F32) for p in parts)
    second = sum(p[half:n, :].astype(F32) for p in parts)
    counts = sum(joined(p[n:, :]) for p in parts)
    keep[0:half, :] = first
    keep[half:, :] = jnp.concatenate([counts, counts], axis=1)
    send[0:half, :] = second.astype(BF)
    send[half:, :] = split_counts(counts)


def half_kernel(keep_in, recv, keep, send):
    half = 2 * TILE
    counts = keep_in[half : half + 8, 0:TILE] + joined(recv[half:, :])[2:10]
    counts = jnp.concatenate([counts, counts], axis=0)
    keep[0:TILE, :] = keep_in[0:TILE, :] + recv[0:TILE, :].astype(F32)
    keep[TILE:, :] = jnp.concatenate([counts, counts], axis=1)
    send[0:TILE, :] = (keep_in[TILE:half, :] + recv[TILE:half, :].astype(F32)).astype(BF)
    send[TILE:, :] = split_counts(counts)


def degree_column(row):
    eye = lax.broadcasted_iota(jnp.int32, (TILE, TILE), 0) == lax.broadcasted_iota(
        jnp.int32, (TILE, TILE), 1
    )
    wide = jnp.broadcast_to(row, (TILE, TILE))
    return jnp.sum(jnp.where(eye, wide, 0.0), axis=1, keepdims=True)


def node_kernel(
    keep, recv, in_degree, features, w_self, w_neigh, bias, grad_out,
    hidden, aggregate, grad_pre, scaled,
):
    neigh = keep[0:TILE, :] + recv[0:TILE, :].astype(F32)
    edges = keep[TILE : TILE + 1, 0:TILE] + joined(recv[TILE:, :])[1:2]
    degree = degree_column(edges + in_degree[...].astype(F32))
    mean = (neigh / degree).astype(BF)
    aggregate[...] = mean
    v = (
        jnp.dot(features[...], w_self[...], preferred_element_type=F32)
        + jnp.dot(mean, w_neigh[...], preferred_element_type=F32)
        + bias[...]
    )
    c = 0.7978845608028654
    t = jnp.tanh(c * (v + 0.044715 * v * v * v))
    hidden[...] = (0.5 * v * (1.0 + t)).astype(BF)
    slope = 0.5 * (1.0 + t) + 0.5 * v * (1.0 - t * t) * (c * (1.0 + 3.0 * 0.044715 * v * v))
    g = (grad_out[...].astype(F32) * slope).astype(BF)
    grad_pre[...] = g
    back = lax.dot_general(g, w_neigh[...], (((1,), (1,)), ((), ())), preferred_element_type=F32)
    scaled[...] = (back / degree).astype(BF)


def weight_kernel(size, features, aggregate, grad_pre, w_self, cuts, self_back):
    g = grad_pre[...]
    contract = (((0,), (0,)), ((), ()))
    first = lax.dot_general(features[...], g, contract, preferred_element_type=F32)
    second = lax.dot_general(aggregate[...], g, contract, preferred_element_type=F32)
    bias = jnp.broadcast_to(jnp.sum(g.astype(F32), axis=0, keepdims=True), (PIECE - 64, HID))
    rows = HID // size
    for i in range(size):
        for j, terms in enumerate((first, second)):
            at = (i * 2 + j) * PIECE
            cuts[at : at + rows, :] = terms[i * rows : (i + 1) * rows].astype(BF)
            cuts[at + rows : at + PIECE, :] = bias[0 : PIECE - rows].astype(BF)
    self_back[...] = lax.dot_general(
        g, w_self[...], (((1,), (1,)), ((), ())), preferred_element_type=F32
    )


def two_terms(value):
    hi = value.astype(BF)
    return jnp.concatenate([hi, (value - hi.astype(F32)).astype(BF)], axis=0)


def one_value(terms):
    return terms[0:PIECE].astype(F32) + terms[PIECE:].astype(F32)


def pair_kernel(own, recv, cuts, out):
    out[0:TILE, :] = own[...]
    out[TILE : 2 * TILE, :] = recv[...]
    pieces = [cuts[i : i + PIECE, :].astype(F32) for i in range(0, cuts.shape[0], PIECE)]
    out[2 * TILE :, :] = sum(pieces).astype(BF)


def quad_kernel(own, recv, out):
    n = 2 * TILE
    out[0:n, :] = own[0:n, :]
    out[n : 2 * n, :] = recv[0:n, :]
    out[2 * n :, :] = two_terms(own[n:, :].astype(F32) + recv[n:, :].astype(F32))


def piece_kernel(own, recv, out):
    n = own.shape[0] - 2 * PIECE
    out[...] = (one_value(own[n:, :]) + one_value(recv[n:, :])).astype(BF)


def pick_kernel(slots, chunks, idx, place, *refs):
    blocks, (msg, held) = refs[:chunks], refs[chunks:]
    for s in range(slots):
        for o in range(chunks):

            @pl.when((idx[s] >= 0) & (idx[s] // QUAD == o))
            def _():
                at = pl.multiple_of((idx[s] % QUAD) * TILE, TILE)
                msg[s * TILE : (s + 1) * TILE, :] = blocks[o][pl.ds(at, TILE), :]

        @pl.when(idx[s] < 0)
        def _():
            msg[s * TILE : (s + 1) * TILE, :] = jnp.zeros((TILE, HID), BF)

    for o in range(chunks):
        held[lax.rem(place[0] + o, chunks)] = one_value(blocks[o][QUAD * TILE :, :])
    msg[slots * TILE :, :] = two_terms(sum(held[o] for o in range(chunks)))


def back_kernel(slots, chunks, src, idx, live, tiles, recv, *refs):
    blocks, (keep, send, acc, got) = refs[:chunks], refs[chunks:]
    acc[...] = jnp.zeros_like(acc)
    for s in range(slots):

        @pl.when(live[s] > 0)
        def _():
            for o in range(chunks):

                @pl.when((idx[s] >= 0) & (idx[s] // QUAD == o))
                def _():
                    at = pl.multiple_of((idx[s] % QUAD) * TILE, TILE)
                    got[...] = blocks[o][pl.ds(at, TILE), :]

            @pl.when(idx[s] < 0)
            def _():
                got[...] = recv[s * TILE : (s + 1) * TILE, :]

            term = lax.dot_general(
                tiles[s], got[...], (((0,), (0,)), ((), ())), preferred_element_type=F32
            )
            to = pl.multiple_of(src[s] * TILE, TILE)
            acc[pl.ds(to, TILE), :] += term

    half = keep.shape[0]
    keep[...] = acc[0:half, :]
    send[...] = acc[half:, :].astype(BF)


def back_cut_kernel(keep_in, recv, piece_in, other, keep, piece, *sends):
    piece[...] = (piece_in[...].astype(F32) + other[...].astype(F32)).astype(BF)
    rows = keep.shape[0]
    for d, ref in enumerate((keep,) + sends):
        at = d * rows
        got = keep_in[at : at + rows, :] + recv[at : at + rows, :].astype(F32)
        ref[...] = got.astype(ref.dtype)


def back_gather_kernel(size, near, piece, *refs):
    recvs, (keep, send) = refs[: size - 1], refs[size - 1 :]
    total = near[...] + sum(r[...].astype(F32) for r in recvs)
    keep[...] = total[0:TILE]
    send[0:TILE, :] = total[total.shape[0] - TILE :].astype(BF)
    send[TILE:, :] = piece[...]


def copies_kernel(own, far, out):
    total = (own[TILE:, :].astype(F32) + far[TILE:, :].astype(F32)).astype(BF)
    for i in range(0, out.shape[0], PIECE):
        out[i : i + PIECE, :] = total


def last_kernel(size, self_back, near, far, pieces, grads, first, second, bias):
    grads[...] = (self_back[...] + near[...] + far[0:TILE, :].astype(F32)).astype(BF)
    rows = HID // size
    for i in range(size):
        for j, ref in enumerate((first, second)):
            at = (i * 2 + j) * PIECE
            ref[i * rows : (i + 1) * rows, :] = pieces[at : at + rows, :].astype(F32)
    bias[...] = pieces[rows : rows + 8, :].astype(F32)[0:1]


def body(
    features,
    tile_values,
    tile_block_row,
    tile_block_col,
    tile_count,
    in_degree,
    w_self,
    w_neigh,
    bias,
    grad_out,
):
    nh, nx, nk, ny, nl = (lax.axis_size(a) for a in ("h", "x", "k", "y", "l"))
    h, x, k, y, l = (lax.axis_index(a) for a in ("h", "x", "k", "y", "l"))
    slots = tile_values.shape[2]
    sources = nh * nx * nk

    def flip(value, axis, bit):
        n = lax.axis_size(axis)
        return lax.ppermute(value, axis, [(i, i ^ bit) for i in range(n)])

    def shift(value, axis, by):
        n = lax.axis_size(axis)
        return lax.ppermute(value, axis, [(i, (i + by) % n) for i in range(n)])

    slot = jnp.arange(slots, dtype=jnp.int32)
    live = (slot < tile_count[0, 0]).astype(jnp.int32)
    dest = jnp.where(live > 0, tile_block_row[0, 0], -1)
    source = tile_block_col[0, 0]
    sh, sx, sk = source // (nx * nk), (source // nk) % nx, source % nk
    src = ((sk ^ k) * nx + (sx - x) % nx) * nh + (sh ^ h)

    def place(d):
        dl = d % nl
        far = (dl >> 1) ^ (l >> 1)
        lay = ((far & 1) << 1) | (far >> 1)
        mine = (d >= 0) & ((dl & 1) == (l & 1))
        return jnp.where(mine, ((d // nl - y) % ny) * QUAD + lay, -1)

    meta = jnp.zeros((8, TILE), jnp.int32).at[0, :slots].set(dest)
    other = flip(meta, "l", 1)[0, :slots]
    own_idx, other_idx = place(dest), place(other)
    where = y.astype(jnp.int32)[None]

    panel = features
    if nh > 1:
        panel = jnp.concatenate([panel, flip(panel, "h", 1)], axis=0)
    panel = jnp.concatenate([panel] + [shift(panel, "x", -d) for d in range(1, nx)], axis=0)
    panel = jnp.concatenate([panel, flip(panel, "k", 1)], axis=0)

    tile_flops = 2 * slots * TILE * TILE * HID
    msg, tiles = call(
        functools.partial(contrib_kernel, slots),
        [((slots * TILE + CNT, HID), BF), ((slots, TILE, TILE), BF)],
        [SMEM, VMEM, VMEM],
        src,
        tile_values[0, 0],
        panel,
        flops=tile_flops,
    )
    chunks = call(
        functools.partial(merge_kernel, slots, ny),
        [((CHUNK, HID), BF)] * ny,
        [SMEM, SMEM, SMEM, VMEM, VMEM, VMEM],
        src,
        own_idx,
        other_idx,
        tiles,
        panel,
        flip(msg, "l", 1),
        scratch=[pltpu.VMEM((ny * CHUNK, HID), F32)],
        flops=tile_flops,
    )

    ups, downs = ny // 2, ny - 1 - ny // 2
    up, down = chunks[ups], chunks[(-downs) % ny]
    parts = [chunks[0]]
    for step in range(1, ups + 1):
        up = shift(up, "y", 1)
        if step <= downs:
            down = shift(down, "y", -1)
        if step < ups:
            (up,) = call(add_kernel, [((CHUNK, HID), BF)], [VMEM] * 2, up, chunks[ups - step])
        if step < downs:
            (down,) = call(
                add_kernel, [((CHUNK, HID), BF)], [VMEM] * 2, down, chunks[ny - downs + step]
            )
    parts.append(up)
    if downs:
        parts.append(down)
    half_rows, last_rows = 2 * TILE + CNT, TILE + CNT
    keep, send = call(
        ring_end_kernel,
        [((half_rows, HID), F32), ((half_rows, HID), BF)],
        [VMEM] * len(parts),
        *parts,
    )
    keep, send = call(
        half_kernel,
        [((last_rows, HID), F32), ((last_rows, HID), BF)],
        [VMEM] * 2,
        keep,
        flip(send, "l", 2),
    )
    node = ((TILE, HID), BF)
    hidden, aggregate, grad_pre, scaled = call(
        node_kernel,
        [node] * 4,
        [VMEM] * 8,
        keep,
        flip(send, "l", 4),
        in_degree.reshape(1, TILE),
        features,
        w_self,
        w_neigh,
        bias.reshape(1, HID),
        grad_out,
        flops=6 * TILE * HID * HID,
    )

    cuts, self_back = call(
        functools.partial(weight_kernel, nx),
        [((nx * nk * PIECE, HID), BF), ((TILE, HID), F32)],
        [VMEM] * 4,
        features,
        aggregate,
        grad_pre,
        w_self,
        flops=6 * TILE * HID * HID,
    )
    cuts = lax.all_to_all(cuts, ("x", "k"), split_axis=0, concat_axis=0, tiled=True)

    (packed,) = call(
        pair_kernel,
        [((2 * TILE + PIECE, HID), BF)],
        [VMEM] * 3,
        scaled,
        flip(scaled, "l", 4),
        cuts,
    )
    (packed,) = call(
        quad_kernel,
        [((4 * TILE + 2 * PIECE, HID), BF)],
        [VMEM] * 2,
        packed,
        flip(packed, "l", 2),
    )
    blocks = [packed] * ny
    up = down = packed
    for step in range(1, ups + 1):
        up = shift(up, "y", 1)
        blocks[(-step) % ny] = up
        if step <= downs:
            down = shift(down, "y", -1)
            blocks[step] = down
    (msg,) = call(
        functools.partial(pick_kernel, slots, ny),
        [((slots * TILE + 2 * PIECE, HID), BF)],
        [SMEM, SMEM] + [VMEM] * ny,
        other_idx,
        where,
        *blocks,
        scratch=[pltpu.VMEM((ny, PIECE, HID), F32)],
    )
    got = flip(msg, "l", 1)
    (piece,) = call(piece_kernel, [((PIECE, HID), BF)], [VMEM] * 2, msg, got)

    half = sources // 2 * TILE
    keep, send = call(
        functools.partial(back_kernel, slots, ny),
        [((half, HID), F32), ((half, HID), BF)],
        [SMEM, SMEM, SMEM, VMEM, VMEM] + [VMEM] * ny,
        src,
        own_idx,
        live,
        tiles,
        got,
        *blocks,
        scratch=[pltpu.VMEM((sources * TILE, HID), F32), pltpu.VMEM((TILE, HID), BF)],
        flops=tile_flops,
    )
    group = nh * TILE
    near, piece, *sends = call(
        back_cut_kernel,
        [((group, HID), F32), ((PIECE, HID), BF)] + [((group, HID), BF)] * (nx - 1),
        [VMEM] * 4,
        keep,
        flip(send, "k", 1),
        piece,
        flip(piece, "l", 4),
    )
    near, send = call(
        functools.partial(back_gather_kernel, nx),
        [((TILE, HID), F32), ((TILE + PIECE, HID), BF)],
        [VMEM] * (nx + 1),
        near,
        piece,
        *[shift(sends[d - 1], "x", d) for d in range(1, nx)],
    )
    far = flip(send, "h", 1) if nh > 1 else jnp.zeros_like(send)
    (copies,) = call(copies_kernel, [((nx * nk * PIECE, HID), BF)], [VMEM] * 2, send, far)
    pieces = lax.all_to_all(copies, ("x", "k"), split_axis=0, concat_axis=0, tiled=True)
    grad_features, grad_w_self, grad_w_neigh, grad_bias = call(
        functools.partial(last_kernel, nx),
        [node, ((HID, HID), F32), ((HID, HID), F32), ((1, HID), F32)],
        [VMEM] * 4,
        self_back,
        near,
        far,
        pieces,
    )
    return hidden, grad_features, grad_w_self, grad_w_neigh, grad_bias.reshape(HID)


def on_mesh(mesh):
    row, col = ("h", "x", "k"), ("y", "l")
    nodes = P(row + col, None)
    in_specs = (
        nodes,
        P(row, col, None, None, None),
        P(row, col, None),
        P(row, col, None),
        P(row, col),
        P(row + col),
        P(),
        P(),
        P(),
        nodes,
    )
    out_specs = (nodes, nodes, P(), P(), P())
    return jax.shard_map(body, mesh=mesh, in_specs=in_specs, out_specs=out_specs, check_vma=False)


def solution(mesh):
    devices = mesh.devices.reshape(2, 4, 2, 8, 8)
    return on_mesh(Mesh(devices, ("h", "x", "k", "y", "l")))
```

```python
import functools

import jax
import jax.numpy as jnp
from jax import lax
from jax.experimental import pallas as pl
from jax.experimental.pallas import tpu as pltpu
from jax.sharding import Mesh, PartitionSpec as P

BF = jnp.bfloat16
F32 = jnp.float32
TILE = 128
HID = 256
QUAD = 4
CNT = 16
CHUNK = QUAD * TILE + CNT
VMEM = pl.BlockSpec(memory_space=pltpu.VMEM)
SMEM = pl.BlockSpec(memory_space=pltpu.SMEM)
AFTER = pl.BlockSpec(memory_space=pl.ANY)
PIECE = 80


def call(kernel, out, in_specs, *args, scratch=(), flops=0):
    shapes = [jax.ShapeDtypeStruct(s, t) for s, t in out]
    moved = sum(a.size * a.dtype.itemsize for a in args)
    moved += sum(s.size * s.dtype.itemsize for s in shapes)
    return pl.pallas_call(
        kernel,
        out_shape=shapes,
        in_specs=in_specs,
        out_specs=[VMEM] * len(shapes),
        scratch_shapes=list(scratch),
        compiler_params=pltpu.CompilerParams(vmem_limit_bytes=48 * 1024 * 1024),
        cost_estimate=pl.CostEstimate(flops=flops, bytes_accessed=moved, transcendentals=0),
    )(*args)


def split_counts(n):
    hi = n.astype(BF)
    lo = (n - hi.astype(F32)).astype(BF)
    return jnp.concatenate([hi, lo], axis=1)


def joined(block):
    return block[:, :TILE].astype(F32) + block[:, TILE:].astype(F32)


def row_counts(tile):
    ones = jnp.ones((8, TILE), BF)
    return lax.dot_general(ones, tile, (((1,), (1,)), ((), ())), preferred_element_type=F32)[0:1]


def add_counts(acc, chunk, lay, row):
    at = pl.multiple_of(chunk * CHUNK + QUAD * TILE, 16)
    mine = lax.broadcasted_iota(jnp.int32, (8, TILE), 0) == lay
    acc[pl.ds(at, 8), 0:TILE] += jnp.where(mine, jnp.broadcast_to(row, (8, TILE)), 0.0)


def contrib_kernel(slots, src, tiles, panel, msg, tiles_bf):
    rows = []
    for s in range(slots):
        tile = tiles[s].astype(F32).astype(BF)
        tiles_bf[s] = tile
        at = pl.multiple_of(src[s] * TILE, TILE)
        got = jnp.dot(tile, panel[pl.ds(at, TILE), :], preferred_element_type=F32)
        msg[s * TILE : (s + 1) * TILE, :] = got.astype(BF)
        rows.append(row_counts(tile))
    rows.append(jnp.zeros((CNT - slots, TILE), F32))
    counts = jnp.concatenate(rows, axis=0)
    msg[slots * TILE :, :] = jnp.concatenate([counts, jnp.zeros_like(counts)], axis=1).astype(BF)


def merge_kernel(slots, chunks, src, idx, other_idx, tiles, panel, recv, *refs):
    outs, acc = refs[:-1], refs[-1]
    acc[...] = jnp.zeros_like(acc)
    counts = recv[slots * TILE :, 0:TILE].astype(F32)

    def put(at, tile, row):
        chunk = at // QUAD
        lay = at % QUAD
        to = pl.multiple_of(chunk * CHUNK + lay * TILE, 16)
        acc[pl.ds(to, TILE), :] += tile
        add_counts(acc, chunk, lay, row)

    for s in range(slots):

        @pl.when(idx[s] >= 0)
        def _():
            at = pl.multiple_of(src[s] * TILE, TILE)
            got = jnp.dot(tiles[s], panel[pl.ds(at, TILE), :], preferred_element_type=F32)
            put(idx[s], got, row_counts(tiles[s]))

        @pl.when(other_idx[s] >= 0)
        def _():
            put(
                other_idx[s], recv[s * TILE : (s + 1) * TILE, :].astype(F32), counts[s : s + 1]
            )

    for o in range(chunks):
        at = o * CHUNK
        outs[o][0 : QUAD * TILE, :] = acc[at : at + QUAD * TILE, :].astype(BF)
        outs[o][QUAD * TILE :, :] = split_counts(acc[at + QUAD * TILE : at + CHUNK, 0:TILE])


def add_kernel(recv, own, out):
    n = QUAD * TILE
    out[0:n, :] = (recv[0:n, :].astype(F32) + own[0:n, :].astype(F32)).astype(BF)
    out[n:, :] = split_counts(joined(recv[n:, :]) + joined(own[n:, :]))


def ring_end_kernel(*refs):
    parts, keep, send = refs[:-2], refs[-2], refs[-1]
    half, n = 2 * TILE, QUAD * TILE
    first = sum(p[0:half, :].astype(F32) for p in parts)
    second = sum(p[half:n, :].astype(F32) for p in parts)
    counts = sum(joined(p[n:, :]) for p in parts)
    keep[0:half, :] = first
    keep[half:, :] = jnp.concatenate([counts, counts], axis=1)
    send[0:half, :] = second.astype(BF)
    send[half:, :] = split_counts(counts)


def half_kernel(keep_in, recv, keep, send):
    half = 2 * TILE
    counts = keep_in[half : half + 8, 0:TILE] + joined(recv[half:, :])[2:10]
    counts = jnp.concatenate([counts, counts], axis=0)
    keep[0:TILE, :] = keep_in[0:TILE, :] + recv[0:TILE, :].astype(F32)
    keep[TILE:, :] = jnp.concatenate([counts, counts], axis=1)
    send[0:TILE, :] = (keep_in[TILE:half, :] + recv[TILE:half, :].astype(F32)).astype(BF)
    send[TILE:, :] = split_counts(counts)


def degree_column(row):
    eye = lax.broadcasted_iota(jnp.int32, (TILE, TILE), 0) == lax.broadcasted_iota(
        jnp.int32, (TILE, TILE), 1
    )
    wide = jnp.broadcast_to(row, (TILE, TILE))
    return jnp.sum(jnp.where(eye, wide, 0.0), axis=1, keepdims=True)


def node_kernel(
    keep, recv, in_degree, features, w_self, w_neigh, bias, grad_out,
    hidden, aggregate, grad_pre, scaled,
):
    neigh = keep[0:TILE, :] + recv[0:TILE, :].astype(F32)
    edges = keep[TILE : TILE + 1, 0:TILE] + joined(recv[TILE:, :])[1:2]
    degree = degree_column(edges + in_degree[...].astype(F32))
    mean = (neigh / degree).astype(BF)
    aggregate[...] = mean
    v = (
        jnp.dot(features[...], w_self[...], preferred_element_type=F32)
        + jnp.dot(mean, w_neigh[...], preferred_element_type=F32)
        + bias[...]
    )
    c = 0.7978845608028654
    t = jnp.tanh(c * (v + 0.044715 * v * v * v))
    hidden[...] = (0.5 * v * (1.0 + t)).astype(BF)
    slope = 0.5 * (1.0 + t) + 0.5 * v * (1.0 - t * t) * (c * (1.0 + 3.0 * 0.044715 * v * v))
    g = (grad_out[...].astype(F32) * slope).astype(BF)
    grad_pre[...] = g
    back = lax.dot_general(g, w_neigh[...], (((1,), (1,)), ((), ())), preferred_element_type=F32)
    scaled[...] = (back / degree).astype(BF)


def weight_kernel(size, features, aggregate, grad_pre, w_self, cuts, self_back):
    g = grad_pre[...]
    contract = (((0,), (0,)), ((), ()))
    first = lax.dot_general(features[...], g, contract, preferred_element_type=F32)
    second = lax.dot_general(aggregate[...], g, contract, preferred_element_type=F32)
    bias = jnp.broadcast_to(jnp.sum(g.astype(F32), axis=0, keepdims=True), (PIECE - 64, HID))
    rows = HID // size
    for i in range(size):
        for j, terms in enumerate((first, second)):
            at = (i * 2 + j) * PIECE
            cuts[at : at + rows, :] = terms[i * rows : (i + 1) * rows].astype(BF)
            cuts[at + rows : at + PIECE, :] = bias[0 : PIECE - rows].astype(BF)
    self_back[...] = lax.dot_general(
        g, w_self[...], (((1,), (1,)), ((), ())), preferred_element_type=F32
    )


def pair_kernel(own, recv, cuts, out):
    out[0:TILE, :] = own[...]
    out[TILE : 2 * TILE, :] = recv[...]
    pieces = [cuts[i : i + PIECE, :].astype(F32) for i in range(0, cuts.shape[0], PIECE)]
    out[2 * TILE :, :] = sum(pieces).astype(BF)


def quad_kernel(own, recv, out, piece):
    n = 2 * TILE
    out[0:n, :] = own[0:n, :]
    out[n:, :] = recv[0:n, :]
    piece[...] = (own[n:, :].astype(F32) + recv[n:, :].astype(F32)).astype(BF)


def pass_kernel(block, own, other, out, total):
    out[...] = block[...]
    total[...] = (own[...].astype(F32) + other[...].astype(F32)).astype(total.dtype)


def pick_kernel(slots, chunks, idx, *refs):
    blocks, msg = refs[:chunks], refs[chunks]
    for s in range(slots):
        for o in range(chunks):

            @pl.when((idx[s] >= 0) & (idx[s] // QUAD == o))
            def _():
                at = pl.multiple_of((idx[s] % QUAD) * TILE, TILE)
                msg[s * TILE : (s + 1) * TILE, :] = blocks[o][pl.ds(at, TILE), :]

        @pl.when(idx[s] < 0)
        def _():
            msg[s * TILE : (s + 1) * TILE, :] = jnp.zeros((TILE, HID), BF)


def back_kernel(slots, chunks, src, idx, live, tiles, recv, after, *refs):
    blocks, (keep, send, acc, got) = refs[:chunks], refs[chunks:]
    acc[...] = jnp.zeros_like(acc)
    for s in range(slots):

        @pl.when(live[s] > 0)
        def _():
            for o in range(chunks):

                @pl.when((idx[s] >= 0) & (idx[s] // QUAD == o))
                def _():
                    at = pl.multiple_of((idx[s] % QUAD) * TILE, TILE)
                    got[...] = blocks[o][pl.ds(at, TILE), :]

            @pl.when(idx[s] < 0)
            def _():
                got[...] = recv[s * TILE : (s + 1) * TILE, :]

            term = lax.dot_general(
                tiles[s], got[...], (((0,), (0,)), ((), ())), preferred_element_type=F32
            )
            to = pl.multiple_of(src[s] * TILE, TILE)
            acc[pl.ds(to, TILE), :] += term

    half = keep.shape[0]
    keep[...] = acc[0:half, :]
    send[...] = acc[half:, :].astype(BF)


def back_cut_kernel(keep_in, recv, piece_in, far_piece, keep, piece, *sends):
    piece[...] = (piece_in[...].astype(F32) + far_piece[...].astype(F32)).astype(BF)
    rows = keep.shape[0]
    for d, ref in enumerate((keep,) + sends):
        at = d * rows
        got = keep_in[at : at + rows, :] + recv[at : at + rows, :].astype(F32)
        ref[0:rows, :] = got.astype(ref.dtype)
        if d:
            ref[rows:, :] = piece[...]


def back_gather_kernel(size, place, near, piece, *refs):
    recvs, (whole, *outs) = refs[: size - 1], refs[size - 1 :]
    rows, n = HID // size, near.shape[0]
    for d, ref in enumerate(outs):
        at = slice(d * TILE, (d + 1) * TILE)
        ref[...] = (near[at, :] + sum(r[at, :].astype(F32) for r in recvs)).astype(ref.dtype)
    for d in range(size):
        at = lax.rem(place[1] + size - d, size)
        block = piece[...] if d == 0 else recvs[d - 1][n:, :]
        whole[pl.ds(pl.multiple_of(at * rows, 16), rows), :] = block[0:rows, :]

        @pl.when(at == 0)
        def _():
            whole[HID:, :] = block[rows:, :]


def last_kernel(place, self_back, near, far, whole, across, grads, first, second, bias):
    grads[...] = (self_back[...] + near[...] + far[...].astype(F32)).astype(BF)
    mine, other = whole[...].astype(F32), across[...].astype(F32)
    own = place[0] == 0
    first[...] = jnp.where(own, mine[0:HID], other[0:HID])
    second[...] = jnp.where(own, other[0:HID], mine[0:HID])
    bias[...] = jnp.where(own, mine[HID : HID + 1], other[HID : HID + 1])


def body(
    features,
    tile_values,
    tile_block_row,
    tile_block_col,
    tile_count,
    in_degree,
    w_self,
    w_neigh,
    bias,
    grad_out,
):
    nh, nx, nk, ny, nl = (lax.axis_size(a) for a in ("h", "x", "k", "y", "l"))
    h, x, k, y, l = (lax.axis_index(a) for a in ("h", "x", "k", "y", "l"))
    slots = tile_values.shape[2]
    sources = nh * nx * nk

    def flip(value, axis, bit):
        n = lax.axis_size(axis)
        return lax.ppermute(value, axis, [(i, i ^ bit) for i in range(n)])

    def shift(value, axis, by):
        n = lax.axis_size(axis)
        return lax.ppermute(value, axis, [(i, (i + by) % n) for i in range(n)])

    slot = jnp.arange(slots, dtype=jnp.int32)
    live = (slot < tile_count[0, 0]).astype(jnp.int32)
    dest = jnp.where(live > 0, tile_block_row[0, 0], -1)
    source = tile_block_col[0, 0]
    sh, sx, sk = source // (nx * nk), (source // nk) % nx, source % nk
    src = ((sk ^ k) * nx + (sx - x) % nx) * nh + (sh ^ h)

    def place(d):
        dl = d % nl
        far = (dl >> 1) ^ (l >> 1)
        lay = ((far & 1) << 1) | (far >> 1)
        mine = (d >= 0) & ((dl & 1) == (l & 1))
        return jnp.where(mine, ((d // nl - y) % ny) * QUAD + lay, -1)

    meta = jnp.zeros((8, TILE), jnp.int32).at[0, :slots].set(dest)
    other = flip(meta, "l", 1)[0, :slots]
    own_idx, other_idx = place(dest), place(other)
    where = jnp.stack([k, x]).astype(jnp.int32)

    panel = features
    if nh > 1:
        panel = jnp.concatenate([panel, flip(panel, "h", 1)], axis=0)
    panel = jnp.concatenate([panel] + [shift(panel, "x", -d) for d in range(1, nx)], axis=0)
    panel = jnp.concatenate([panel, flip(panel, "k", 1)], axis=0)

    tile_flops = 2 * slots * TILE * TILE * HID
    msg, tiles = call(
        functools.partial(contrib_kernel, slots),
        [((slots * TILE + CNT, HID), BF), ((slots, TILE, TILE), BF)],
        [SMEM, VMEM, VMEM],
        src,
        tile_values[0, 0],
        panel,
        flops=tile_flops,
    )
    chunks = call(
        functools.partial(merge_kernel, slots, ny),
        [((CHUNK, HID), BF)] * ny,
        [SMEM, SMEM, SMEM, VMEM, VMEM, VMEM],
        src,
        own_idx,
        other_idx,
        tiles,
        panel,
        flip(msg, "l", 1),
        scratch=[pltpu.VMEM((ny * CHUNK, HID), F32)],
        flops=tile_flops,
    )

    ups, downs = ny // 2, ny - 1 - ny // 2
    up, down = chunks[ups], chunks[(-downs) % ny]
    parts = [chunks[0]]
    for step in range(1, ups + 1):
        up = shift(up, "y", 1)
        if step <= downs:
            down = shift(down, "y", -1)
        if step < ups:
            (up,) = call(add_kernel, [((CHUNK, HID), BF)], [VMEM] * 2, up, chunks[ups - step])
        if step < downs:
            (down,) = call(
                add_kernel, [((CHUNK, HID), BF)], [VMEM] * 2, down, chunks[ny - downs + step]
            )
    parts.append(up)
    if downs:
        parts.append(down)
    half_rows, last_rows = 2 * TILE + CNT, TILE + CNT
    keep, send = call(
        ring_end_kernel,
        [((half_rows, HID), F32), ((half_rows, HID), BF)],
        [VMEM] * len(parts),
        *parts,
    )
    keep, send = call(
        half_kernel,
        [((last_rows, HID), F32), ((last_rows, HID), BF)],
        [VMEM] * 2,
        keep,
        flip(send, "l", 2),
    )
    node = ((TILE, HID), BF)
    hidden, aggregate, grad_pre, scaled = call(
        node_kernel,
        [node] * 4,
        [VMEM] * 8,
        keep,
        flip(send, "l", 4),
        in_degree.reshape(1, TILE),
        features,
        w_self,
        w_neigh,
        bias.reshape(1, HID),
        grad_out,
        flops=6 * TILE * HID * HID,
    )

    cuts, self_back = call(
        functools.partial(weight_kernel, nx),
        [((nx * nk * PIECE, HID), BF), ((TILE, HID), F32)],
        [VMEM] * 4,
        features,
        aggregate,
        grad_pre,
        w_self,
        flops=6 * TILE * HID * HID,
    )
    cuts = lax.all_to_all(cuts, ("x", "k"), split_axis=0, concat_axis=0, tiled=True)

    (packed,) = call(
        pair_kernel,
        [((2 * TILE + PIECE, HID), BF)],
        [VMEM] * 3,
        scaled,
        flip(scaled, "l", 4),
        cuts,
    )
    packed, total = call(
        quad_kernel,
        [((4 * TILE, HID), BF), ((PIECE, HID), BF)],
        [VMEM] * 2,
        packed,
        flip(packed, "l", 2),
    )

    def partner(axis, bit):
        there = bit < lax.axis_size(axis)
        return flip(total, axis, bit) if there else jnp.zeros_like(total)

    sums = [("h", 1, F32), ("l", 4, F32), ("l", 1, F32)]
    blocks = [packed] * ny
    up = down = packed
    for step in range(1, ups + 1):
        up = shift(up, "y", 1)
        if step <= downs:
            down = shift(down, "y", -1)
            blocks[step] = down
        if step < ups and sums:
            axis, bit, kind = sums.pop(0)
            up, total = call(
                pass_kernel,
                [((4 * TILE, HID), BF), ((PIECE, HID), kind)],
                [VMEM] * 3,
                up,
                total,
                partner(axis, bit),
            )
        blocks[(-step) % ny] = up
    for axis, bit, kind in sums:
        total = (total.astype(F32) + partner(axis, bit).astype(F32)).astype(kind)
    (msg,) = call(
        functools.partial(pick_kernel, slots, ny),
        [((slots * TILE, HID), BF)],
        [SMEM] + [VMEM] * ny,
        other_idx,
        *blocks,
    )
    got = flip(msg, "l", 1)
    total = total + partner("y", 1)
    total = total + partner("y", 2)

    half = sources // 2 * TILE
    keep, send = call(
        functools.partial(back_kernel, slots, ny),
        [((half, HID), F32), ((half, HID), BF)],
        [SMEM, SMEM, SMEM, VMEM, VMEM, AFTER] + [VMEM] * ny,
        src,
        own_idx,
        live,
        tiles,
        got,
        total,
        *blocks,
        scratch=[pltpu.VMEM((sources * TILE, HID), F32), pltpu.VMEM((TILE, HID), BF)],
        flops=tile_flops,
    )
    group = nh * TILE
    near, piece, *sends = call(
        back_cut_kernel,
        [((group, HID), F32), ((PIECE, HID), BF)] + [((group + PIECE, HID), BF)] * (nx - 1),
        [VMEM] * 4,
        keep,
        flip(send, "k", 1),
        total,
        partner("y", 4),
    )
    whole, *last = call(
        functools.partial(back_gather_kernel, nx),
        [((HID + 16, HID), BF), ((TILE, HID), F32)] + [node] * (nh - 1),
        [SMEM] + [VMEM] * (nx + 1),
        where,
        near,
        piece,
        *[shift(sends[d - 1], "x", d) for d in range(1, nx)],
    )
    far = flip(last[1], "h", 1) if nh > 1 else jnp.zeros((TILE, HID), BF)
    grad_features, grad_w_self, grad_w_neigh, grad_bias = call(
        last_kernel,
        [node, ((HID, HID), F32), ((HID, HID), F32), ((1, HID), F32)],
        [SMEM] + [VMEM] * 5,
        where,
        self_back,
        last[0],
        far,
        whole,
        flip(whole, "k", 1),
    )
    return hidden, grad_features, grad_w_self, grad_w_neigh, grad_bias.reshape(HID)


def on_mesh(mesh):
    row, col = ("h", "x", "k"), ("y", "l")
    nodes = P(row + col, None)
    in_specs = (
        nodes,
        P(row, col, None, None, None),
        P(row, col, None),
        P(row, col, None),
        P(row, col),
        P(row + col),
        P(),
        P(),
        P(),
        nodes,
    )
    out_specs = (nodes, nodes, P(), P(), P())
    return jax.shard_map(body, mesh=mesh, in_specs=in_specs, out_specs=out_specs, check_vma=False)


def solution(mesh):
    devices = mesh.devices.reshape(2, 4, 2, 8, 8)
    return on_mesh(Mesh(devices, ("h", "x", "k", "y", "l")))
```

```python
import functools

import jax
import jax.numpy as jnp
from jax import lax
from jax.experimental import pallas as pl
from jax.experimental.pallas import tpu as pltpu
from jax.sharding import Mesh, PartitionSpec as P

BF = jnp.bfloat16
F32 = jnp.float32
TILE = 128
HID = 256
QUAD = 4
CNT = 16
CHUNK = QUAD * TILE + CNT
VMEM = pl.BlockSpec(memory_space=pltpu.VMEM)
SMEM = pl.BlockSpec(memory_space=pltpu.SMEM)
AFTER = pl.BlockSpec(memory_space=pl.ANY)
PIECE = 80


def call(kernel, out, in_specs, *args, scratch=(), flops=0):
    shapes = [jax.ShapeDtypeStruct(s, t) for s, t in out]
    moved = sum(a.size * a.dtype.itemsize for a in args)
    moved += sum(s.size * s.dtype.itemsize for s in shapes)
    return pl.pallas_call(
        kernel,
        out_shape=shapes,
        in_specs=in_specs,
        out_specs=[VMEM] * len(shapes),
        scratch_shapes=list(scratch),
        compiler_params=pltpu.CompilerParams(vmem_limit_bytes=48 * 1024 * 1024),
        cost_estimate=pl.CostEstimate(flops=flops, bytes_accessed=moved, transcendentals=0),
    )(*args)


def split_counts(n):
    hi = n.astype(BF)
    lo = (n - hi.astype(F32)).astype(BF)
    return jnp.concatenate([hi, lo], axis=1)


def joined(block):
    return block[:, :TILE].astype(F32) + block[:, TILE:].astype(F32)


def row_counts(tile):
    ones = jnp.ones((8, TILE), BF)
    return lax.dot_general(ones, tile, (((1,), (1,)), ((), ())), preferred_element_type=F32)[0:1]


def add_counts(acc, chunk, lay, row):
    at = pl.multiple_of(chunk * CHUNK + QUAD * TILE, 16)
    mine = lax.broadcasted_iota(jnp.int32, (8, TILE), 0) == lay
    acc[pl.ds(at, 8), 0:TILE] += jnp.where(mine, jnp.broadcast_to(row, (8, TILE)), 0.0)


def contrib_kernel(slots, src, tiles, panel, msg, tiles_bf):
    rows = []
    for s in range(slots):
        tile = tiles[s].astype(F32).astype(BF)
        tiles_bf[s] = tile
        at = pl.multiple_of(src[s] * TILE, TILE)
        got = jnp.dot(tile, panel[pl.ds(at, TILE), :], preferred_element_type=F32)
        msg[s * TILE : (s + 1) * TILE, :] = got.astype(BF)
        rows.append(row_counts(tile))
    rows.append(jnp.zeros((CNT - slots, TILE), F32))
    counts = jnp.concatenate(rows, axis=0)
    msg[slots * TILE :, :] = jnp.concatenate([counts, jnp.zeros_like(counts)], axis=1).astype(BF)


def merge_kernel(slots, chunks, src, idx, other_idx, tiles, panel, recv, *refs):
    outs, acc = refs[:-1], refs[-1]
    acc[...] = jnp.zeros_like(acc)
    counts = recv[slots * TILE :, 0:TILE].astype(F32)

    def put(at, tile, row):
        chunk = at // QUAD
        lay = at % QUAD
        to = pl.multiple_of(chunk * CHUNK + lay * TILE, 16)
        acc[pl.ds(to, TILE), :] += tile
        add_counts(acc, chunk, lay, row)

    for s in range(slots):

        @pl.when(idx[s] >= 0)
        def _():
            at = pl.multiple_of(src[s] * TILE, TILE)
            got = jnp.dot(tiles[s], panel[pl.ds(at, TILE), :], preferred_element_type=F32)
            put(idx[s], got, row_counts(tiles[s]))

        @pl.when(other_idx[s] >= 0)
        def _():
            put(
                other_idx[s], recv[s * TILE : (s + 1) * TILE, :].astype(F32), counts[s : s + 1]
            )

    for o in range(chunks):
        at = o * CHUNK
        outs[o][0 : QUAD * TILE, :] = acc[at : at + QUAD * TILE, :].astype(BF)
        outs[o][QUAD * TILE :, :] = split_counts(acc[at + QUAD * TILE : at + CHUNK, 0:TILE])


def add_kernel(recv, own, out):
    n = QUAD * TILE
    out[0:n, :] = (recv[0:n, :].astype(F32) + own[0:n, :].astype(F32)).astype(BF)
    out[n:, :] = split_counts(joined(recv[n:, :]) + joined(own[n:, :]))


def ring_end_kernel(*refs):
    parts, keep, send = refs[:-2], refs[-2], refs[-1]
    half, n = 2 * TILE, QUAD * TILE
    first = sum(p[0:half, :].astype(F32) for p in parts)
    second = sum(p[half:n, :].astype(F32) for p in parts)
    counts = sum(joined(p[n:, :]) for p in parts)
    keep[0:half, :] = first
    keep[half:, :] = jnp.concatenate([counts, counts], axis=1)
    send[0:half, :] = second.astype(BF)
    send[half:, :] = split_counts(counts)


def half_kernel(keep_in, recv, keep, send):
    half = 2 * TILE
    counts = keep_in[half : half + 8, 0:TILE] + joined(recv[half:, :])[2:10]
    counts = jnp.concatenate([counts, counts], axis=0)
    keep[0:TILE, :] = keep_in[0:TILE, :] + recv[0:TILE, :].astype(F32)
    keep[TILE:, :] = jnp.concatenate([counts, counts], axis=1)
    send[0:TILE, :] = (keep_in[TILE:half, :] + recv[TILE:half, :].astype(F32)).astype(BF)
    send[TILE:, :] = split_counts(counts)


def degree_column(row):
    eye = lax.broadcasted_iota(jnp.int32, (TILE, TILE), 0) == lax.broadcasted_iota(
        jnp.int32, (TILE, TILE), 1
    )
    wide = jnp.broadcast_to(row, (TILE, TILE))
    return jnp.sum(jnp.where(eye, wide, 0.0), axis=1, keepdims=True)


def node_kernel(
    keep, recv, in_degree, features, w_self, w_neigh, bias, grad_out,
    hidden, aggregate, grad_pre, scaled,
):
    neigh = keep[0:TILE, :] + recv[0:TILE, :].astype(F32)
    edges = keep[TILE : TILE + 1, 0:TILE] + joined(recv[TILE:, :])[1:2]
    degree = degree_column(edges + in_degree[...].astype(F32))
    mean = (neigh / degree).astype(BF)
    aggregate[...] = mean
    v = (
        jnp.dot(features[...], w_self[...], preferred_element_type=F32)
        + jnp.dot(mean, w_neigh[...], preferred_element_type=F32)
        + bias[...]
    )
    c = 0.7978845608028654
    t = jnp.tanh(c * (v + 0.044715 * v * v * v))
    hidden[...] = (0.5 * v * (1.0 + t)).astype(BF)
    slope = 0.5 * (1.0 + t) + 0.5 * v * (1.0 - t * t) * (c * (1.0 + 3.0 * 0.044715 * v * v))
    g = (grad_out[...].astype(F32) * slope).astype(BF)
    grad_pre[...] = g
    back = lax.dot_general(g, w_neigh[...], (((1,), (1,)), ((), ())), preferred_element_type=F32)
    scaled[...] = (back / degree).astype(BF)


def weight_kernel(size, features, aggregate, grad_pre, w_self, cuts, self_back):
    g = grad_pre[...]
    contract = (((0,), (0,)), ((), ()))
    first = lax.dot_general(features[...], g, contract, preferred_element_type=F32)
    second = lax.dot_general(aggregate[...], g, contract, preferred_element_type=F32)
    bias = jnp.broadcast_to(jnp.sum(g.astype(F32), axis=0, keepdims=True), (PIECE - 64, HID))
    rows = HID // size
    for i in range(size):
        for j, terms in enumerate((first, second)):
            at = (i * 2 + j) * PIECE
            cuts[at : at + rows, :] = terms[i * rows : (i + 1) * rows].astype(BF)
            cuts[at + rows : at + PIECE, :] = bias[0 : PIECE - rows].astype(BF)
    self_back[...] = lax.dot_general(
        g, w_self[...], (((1,), (1,)), ((), ())), preferred_element_type=F32
    )


def pair_kernel(own, recv, cuts, out):
    out[0:TILE, :] = own[...]
    out[TILE : 2 * TILE, :] = recv[...]
    pieces = [cuts[i : i + PIECE, :].astype(F32) for i in range(0, cuts.shape[0], PIECE)]
    out[2 * TILE :, :] = sum(pieces).astype(BF)


def quad_kernel(own, recv, out, piece):
    n = 2 * TILE
    out[0:n, :] = own[0:n, :]
    out[n:, :] = recv[0:n, :]
    piece[...] = (own[n:, :].astype(F32) + recv[n:, :].astype(F32)).astype(BF)


def pass_kernel(block, own, other, out, total):
    out[...] = block[...]
    total[...] = (own[...].astype(F32) + other[...].astype(F32)).astype(total.dtype)


def pick_kernel(slots, chunks, idx, *refs):
    blocks, msg = refs[:chunks], refs[chunks]
    for s in range(slots):
        for o in range(chunks):

            @pl.when((idx[s] >= 0) & (idx[s] // QUAD == o))
            def _():
                at = pl.multiple_of((idx[s] % QUAD) * TILE, TILE)
                msg[s * TILE : (s + 1) * TILE, :] = blocks[o][pl.ds(at, TILE), :]

        @pl.when(idx[s] < 0)
        def _():
            msg[s * TILE : (s + 1) * TILE, :] = jnp.zeros((TILE, HID), BF)


def back_kernel(slots, chunks, src, idx, live, tiles, recv, after, *refs):
    blocks, (keep, send, acc, got) = refs[:chunks], refs[chunks:]
    acc[...] = jnp.zeros_like(acc)
    for s in range(slots):

        @pl.when(live[s] > 0)
        def _():
            for o in range(chunks):

                @pl.when((idx[s] >= 0) & (idx[s] // QUAD == o))
                def _():
                    at = pl.multiple_of((idx[s] % QUAD) * TILE, TILE)
                    got[...] = blocks[o][pl.ds(at, TILE), :]

            @pl.when(idx[s] < 0)
            def _():
                got[...] = recv[s * TILE : (s + 1) * TILE, :]

            term = lax.dot_general(
                tiles[s], got[...], (((0,), (0,)), ((), ())), preferred_element_type=F32
            )
            to = pl.multiple_of(src[s] * TILE, TILE)
            acc[pl.ds(to, TILE), :] += term

    half = keep.shape[0]
    keep[...] = acc[0:half, :]
    send[...] = acc[half:, :].astype(BF)


def back_cut_kernel(keep_in, recv, piece_in, far_piece, keep, piece, *sends):
    piece[...] = (piece_in[...].astype(F32) + far_piece[...].astype(F32)).astype(BF)
    rows = keep.shape[0]
    for d, ref in enumerate((keep,) + sends):
        at = d * rows
        got = keep_in[at : at + rows, :] + recv[at : at + rows, :].astype(F32)
        ref[0:rows, :] = got.astype(ref.dtype)
        if d:
            ref[rows:, :] = piece[...]


def back_gather_kernel(size, place, near, piece, *refs):
    recvs, (whole, *outs) = refs[: size - 1], refs[size - 1 :]
    rows, n = HID // size, near.shape[0]
    for d, ref in enumerate(outs):
        at = slice(d * TILE, (d + 1) * TILE)
        ref[...] = (near[at, :] + sum(r[at, :].astype(F32) for r in recvs)).astype(ref.dtype)
    for d in range(size):
        at = lax.rem(place[1] + size - d, size)
        block = piece[...] if d == 0 else recvs[d - 1][n:, :]
        whole[pl.ds(pl.multiple_of(at * rows, 16), rows), :] = block[0:rows, :]

        @pl.when(at == 0)
        def _():
            whole[HID:, :] = block[rows:, :]


def last_kernel(place, self_back, near, far, whole, across, grads, first, second, bias):
    grads[...] = (self_back[...] + near[...] + far[...].astype(F32)).astype(BF)
    mine, other = whole[...].astype(F32), across[...].astype(F32)
    own = place[0] == 0
    first[...] = jnp.where(own, mine[0:HID], other[0:HID])
    second[...] = jnp.where(own, other[0:HID], mine[0:HID])
    bias[...] = jnp.where(own, mine[HID : HID + 1], other[HID : HID + 1])


def body(
    features,
    tile_values,
    tile_block_row,
    tile_block_col,
    tile_count,
    in_degree,
    w_self,
    w_neigh,
    bias,
    grad_out,
):
    nh, nx, nk, ny, nl = (lax.axis_size(a) for a in ("h", "x", "k", "y", "l"))
    h, x, k, y, l = (lax.axis_index(a) for a in ("h", "x", "k", "y", "l"))
    slots = tile_values.shape[2]
    sources = nh * nx * nk

    def flip(value, axis, bit):
        n = lax.axis_size(axis)
        return lax.ppermute(value, axis, [(i, i ^ bit) for i in range(n)])

    def shift(value, axis, by):
        n = lax.axis_size(axis)
        return lax.ppermute(value, axis, [(i, (i + by) % n) for i in range(n)])

    slot = jnp.arange(slots, dtype=jnp.int32)
    live = (slot < tile_count[0, 0]).astype(jnp.int32)
    dest = jnp.where(live > 0, tile_block_row[0, 0], -1)
    source = tile_block_col[0, 0]
    sh, sx, sk = source // (nx * nk), (source // nk) % nx, source % nk
    src = ((sk ^ k) * nx + (sx - x) % nx) * nh + (sh ^ h)

    def place(d):
        dl = d % nl
        far = (dl >> 1) ^ (l >> 1)
        lay = ((far & 1) << 1) | (far >> 1)
        mine = (d >= 0) & ((dl & 1) == (l & 1))
        return jnp.where(mine, ((d // nl - y) % ny) * QUAD + lay, -1)

    meta = jnp.zeros((8, TILE), jnp.int32).at[0, :slots].set(dest)
    other = flip(meta, "l", 1)[0, :slots]
    own_idx, other_idx = place(dest), place(other)
    where = jnp.stack([k, x]).astype(jnp.int32)

    panel = features
    if nh > 1:
        panel = jnp.concatenate([panel, flip(panel, "h", 1)], axis=0)
    panel = jnp.concatenate([panel] + [shift(panel, "x", -d) for d in range(1, nx)], axis=0)
    panel = jnp.concatenate([panel, flip(panel, "k", 1)], axis=0)

    tile_flops = 2 * slots * TILE * TILE * HID
    msg, tiles = call(
        functools.partial(contrib_kernel, slots),
        [((slots * TILE + CNT, HID), BF), ((slots, TILE, TILE), BF)],
        [SMEM, VMEM, VMEM],
        src,
        tile_values[0, 0],
        panel,
        flops=tile_flops,
    )
    chunks = call(
        functools.partial(merge_kernel, slots, ny),
        [((CHUNK, HID), BF)] * ny,
        [SMEM, SMEM, SMEM, VMEM, VMEM, VMEM],
        src,
        own_idx,
        other_idx,
        tiles,
        panel,
        flip(msg, "l", 1),
        scratch=[pltpu.VMEM((ny * CHUNK, HID), F32)],
        flops=tile_flops,
    )

    ups, downs = ny // 2, ny - 1 - ny // 2
    up, down = chunks[ups], chunks[(-downs) % ny]
    parts = [chunks[0]]
    for step in range(1, ups + 1):
        up = shift(up, "y", 1)
        if step <= downs:
            down = shift(down, "y", -1)
        if step < ups:
            (up,) = call(add_kernel, [((CHUNK, HID), BF)], [VMEM] * 2, up, chunks[ups - step])
        if step < downs:
            (down,) = call(
                add_kernel, [((CHUNK, HID), BF)], [VMEM] * 2, down, chunks[ny - downs + step]
            )
    parts.append(up)
    if downs:
        parts.append(down)
    half_rows, last_rows = 2 * TILE + CNT, TILE + CNT
    keep, send = call(
        ring_end_kernel,
        [((half_rows, HID), F32), ((half_rows, HID), BF)],
        [VMEM] * len(parts),
        *parts,
    )
    keep, send = call(
        half_kernel,
        [((last_rows, HID), F32), ((last_rows, HID), BF)],
        [VMEM] * 2,
        keep,
        flip(send, "l", 2),
    )
    node = ((TILE, HID), BF)
    hidden, aggregate, grad_pre, scaled = call(
        node_kernel,
        [node] * 4,
        [VMEM] * 8,
        keep,
        flip(send, "l", 4),
        in_degree.reshape(1, TILE),
        features,
        w_self,
        w_neigh,
        bias.reshape(1, HID),
        grad_out,
        flops=6 * TILE * HID * HID,
    )

    cuts, self_back = call(
        functools.partial(weight_kernel, nx),
        [((nx * nk * PIECE, HID), BF), ((TILE, HID), F32)],
        [VMEM] * 4,
        features,
        aggregate,
        grad_pre,
        w_self,
        flops=6 * TILE * HID * HID,
    )
    cuts = lax.all_to_all(cuts, ("x", "k"), split_axis=0, concat_axis=0, tiled=True)

    (packed,) = call(
        pair_kernel,
        [((2 * TILE + PIECE, HID), BF)],
        [VMEM] * 3,
        scaled,
        flip(scaled, "l", 4),
        cuts,
    )
    packed, total = call(
        quad_kernel,
        [((4 * TILE, HID), BF), ((PIECE, HID), BF)],
        [VMEM] * 2,
        packed,
        flip(packed, "l", 2),
    )

    def partner(axis, bit):
        there = bit < lax.axis_size(axis)
        return flip(total, axis, bit) if there else jnp.zeros_like(total)

    sums = [("l", 4, F32), ("l", 1, F32), ("y", 1, F32)]
    blocks = [packed] * ny
    up = down = packed
    for step in range(1, ups + 1):
        up = shift(up, "y", 1)
        if step <= downs:
            down = shift(down, "y", -1)
            blocks[step] = down
        if step < ups and sums:
            axis, bit, kind = sums.pop(0)
            up, total = call(
                pass_kernel,
                [((4 * TILE, HID), BF), ((PIECE, HID), kind)],
                [VMEM] * 3,
                up,
                total,
                partner(axis, bit),
            )
        blocks[(-step) % ny] = up
    for axis, bit, kind in sums:
        total = (total.astype(F32) + partner(axis, bit).astype(F32)).astype(kind)
    (msg,) = call(
        functools.partial(pick_kernel, slots, ny),
        [((slots * TILE, HID), BF)],
        [SMEM] + [VMEM] * ny,
        other_idx,
        *blocks,
    )
    got = flip(msg, "l", 1)
    total = total + partner("y", 2)
    total = (total + partner("y", 4)).astype(BF)

    half = sources // 2 * TILE
    keep, send = call(
        functools.partial(back_kernel, slots, ny),
        [((half, HID), F32), ((half, HID), BF)],
        [SMEM, SMEM, SMEM, VMEM, VMEM, AFTER] + [VMEM] * ny,
        src,
        own_idx,
        live,
        tiles,
        got,
        total,
        *blocks,
        scratch=[pltpu.VMEM((sources * TILE, HID), F32), pltpu.VMEM((TILE, HID), BF)],
        flops=tile_flops,
    )
    group = nh * TILE
    near, piece, *sends = call(
        back_cut_kernel,
        [((group, HID), F32), ((PIECE, HID), BF)] + [((group + PIECE, HID), BF)] * (nx - 1),
        [VMEM] * 4,
        keep,
        flip(send, "k", 1),
        total,
        partner("h", 1),
    )
    whole, *last = call(
        functools.partial(back_gather_kernel, nx),
        [((HID + 16, HID), BF), ((TILE, HID), F32)] + [node] * (nh - 1),
        [SMEM] + [VMEM] * (nx + 1),
        where,
        near,
        piece,
        *[shift(sends[d - 1], "x", d) for d in range(1, nx)],
    )
    far = flip(last[1], "h", 1) if nh > 1 else jnp.zeros((TILE, HID), BF)
    grad_features, grad_w_self, grad_w_neigh, grad_bias = call(
        last_kernel,
        [node, ((HID, HID), F32), ((HID, HID), F32), ((1, HID), F32)],
        [SMEM] + [VMEM] * 5,
        where,
        self_back,
        last[0],
        far,
        whole,
        flip(whole, "k", 1),
    )
    return hidden, grad_features, grad_w_self, grad_w_neigh, grad_bias.reshape(HID)


def on_mesh(mesh):
    row, col = ("h", "x", "k"), ("y", "l")
    nodes = P(row + col, None)
    in_specs = (
        nodes,
        P(row, col, None, None, None),
        P(row, col, None),
        P(row, col, None),
        P(row, col),
        P(row + col),
        P(),
        P(),
        P(),
        nodes,
    )
    out_specs = (nodes, nodes, P(), P(), P())
    return jax.shard_map(body, mesh=mesh, in_specs=in_specs, out_specs=out_specs, check_vma=False)


def solution(mesh):
    devices = mesh.devices.reshape(2, 4, 2, 8, 8)
    return on_mesh(Mesh(devices, ("h", "x", "k", "y", "l")))
```
